256 devices in a mesh: row: 16 (over y, x), col: 16 (over z, core).
Axes of the slice: x: 4, y: 4, z: 8, core: 2. Of those that a mesh axis runs over, the one named last changes fastest.
Arguments:
- leaf_state_map: bfloat16 [1024, 512, 512], P(('row', 'col')), may hold values from -0.1875 to 0.1875
- leaf_input_map: bfloat16 [1024, 512, 256], P(('row', 'col')), may hold values from -0.25 to 0.25
- leaf_weight: bfloat16 [1024], P(('row', 'col')), may hold values from 0.29882812 to 3
- leaf_count: int32 [256], P(('row', 'col')), may hold values from 1 to 4, as said below
- mid_state_map: bfloat16 [256, 512, 512], P(('row', 'col')), may hold values from -0.1875 to 0.1875
- mid_input_map: bfloat16 [256, 512, 256], P(('row', 'col')), may hold values from -0.25 to 0.25
- mid_weight: float32 [256], P(('row', 'col')), may hold values from 0.3 to 3
- mid_parent: int32 [256], P(('row', 'col')), may hold values from 0 to 1, as said below
- up_state_map: bfloat16 [32, 512, 512], P('row'), may hold values from -0.1875 to 0.1875
- up_input_map: bfloat16 [32, 512, 256], P('row'), may hold values from -0.25 to 0.25
- up_weight: float32 [32], P('row'), may hold values from 0.3 to 3
- root_cov: bfloat16 [512, 512], replicated, as said below
- state_cost: float32 [512], replicated, may hold values from 0.3 to 3
- control_cost: float32 [256], replicated, may hold values from 0.3 to 3
- noise_cov: float32 [512], replicated, may hold values from 0.05 to 0.5
Outputs:
- root_gain: bfloat16 [256, 512], replicated
- root_value: bfloat16 [512, 512], replicated
- up_gain: bfloat16 [32, 256, 512], P('row')
- up_value: bfloat16 [32, 512, 512], P('row')
- up_cov: bfloat16 [32, 512, 512], P('row')
- mid_gain: bfloat16 [256, 256, 512], P(('row', 'col'))
- mid_value: bfloat16 [256, 512, 512], P(('row', 'col'))
- mid_cov: bfloat16 [256, 512, 512], P(('row', 'col'))
- leaf_cov: bfloat16 [1024, 512, 512], P(('row', 'col'))
The draws below stay inside these ranges and needn't reach their ends.
Inputs may be any that keep to these rules, and one draw needn't show every extreme that they name: `leaf_count`: the number of live leaves of each section-2 node; some node has 4 in every draw. `mid_parent`: the parent slot of each section-2 node within its row group; every section-1 node has at least one child. `root_cov`: symmetric positive definite.
All inputs are finite; a program needn't handle non-finite values.
Results may differ from the reference program's by a relative error of at most 0.02.
Values may be sent and summed in bfloat16 or wider, within the bound.
A program may use at most 128 MiB of HBM per device.

```python
import math
import jax
import jax.numpy as jnp
from jax import lax

NX = 512
NU = 256
LEAF_DEV = 4
S1_ROW = 2
MIDS = 256
LEAVES = 1024
UPPERS = 32
N_ROW = 16
N_COL = 16


def draw_leaf_count(key, part):
    base_key = jax.random.fold_in(key, 11)
    first_key, second_key, third_key = jax.random.split(base_key, 3)
    single = jax.random.randint(first_key, (MIDS,), 0, 2)
    larger = jax.random.randint(second_key, (MIDS,), 2, LEAF_DEV + 1)
    counts = jnp.where(single == 0, 1, larger)
    busiest = jax.random.randint(third_key, (), 0, MIDS)
    counts = jnp.where(jnp.arange(MIDS) == busiest, LEAF_DEV, counts)
    return counts.astype(jnp.int32)


def draw_mid_parent(key, part):
    base_key = jax.random.fold_in(key, 29)
    column = jnp.arange(MIDS, dtype=jnp.int32) % N_COL
    chosen = jax.random.randint(base_key, (MIDS,), 0, S1_ROW)
    return jnp.where(column < S1_ROW, column, chosen).astype(jnp.int32)


def draw_root_cov(key, part):
    base_key = jax.random.fold_in(key, 7)
    first_key, second_key = jax.random.split(base_key, 2)
    factor = jax.random.normal(first_key, (NX, NX), jnp.float32)
    diagonal = jax.random.uniform(second_key, (NX,), jnp.float32, 0.5, 1.5)
    matrix = 0.5 * jnp.dot(factor, factor.T) / NX + jnp.diag(diagonal)
    return matrix.astype(jnp.bfloat16)


def level_of(rng, extent, cuts, smallest, high):
    level = 1.0
    for position, shards_of in cuts:
        steps = jax.random.uniform(jax.random.fold_in(jax.random.fold_in(rng, 6), position), (shards_of,), jnp.float32, smallest / len(cuts), high / len(cuts))
        level = level * jnp.repeat(jnp.exp(steps), extent[position] // shards_of).reshape((-1,) + (1,) * (len(extent) - 1 - position))
    return level


def centred(rng, shape, scale, most, shards=(), kind=jnp.bfloat16):
    result = scale * jax.random.normal(rng, shape, jnp.float32)
    if shards:
        result = result * level_of(rng, shape, shards, -0.22, 0.18)
    return jnp.clip(result, -most, most).astype(kind)


def setup_inputs(seed: int = 0) -> dict:
    key_list = jax.random.split(jax.random.key(seed), 16)
    return {
        "leaf_state_map": centred(key_list[0], (LEAVES, NX, NX), (2 * NX) ** -0.5, 0.1875, ((0, 256),)),
        "leaf_input_map": centred(key_list[1], (LEAVES, NX, NU), NX ** -0.5, 0.25, ((0, 256),)),
        "leaf_weight": jnp.clip(jnp.exp(math.log(3.0) - 2.306499 * jax.random.uniform(key_list[2], (LEAVES,), jnp.float32) ** level_of(key_list[2], (LEAVES,), ((0, 256),), -0.2, 0.2)), 0.29882812, 3.0).astype(jnp.bfloat16),
        "leaf_count": draw_leaf_count(jax.random.fold_in(key_list[15], 71), 0),
        "mid_state_map": centred(key_list[4], (MIDS, NX, NX), (2 * NX) ** -0.5, 0.1875, ((0, 256),)),
        "mid_input_map": centred(key_list[5], (MIDS, NX, NU), NX ** -0.5, 0.25, ((0, 256),)),
        "mid_weight": jnp.clip(jnp.exp(math.log(3.0) - 2.3025851 * jax.random.uniform(key_list[6], (MIDS,), jnp.float32) ** level_of(key_list[6], (MIDS,), ((0, 256),), -0.2, 0.2)), 0.3, 3.0),
        "mid_parent": draw_mid_parent(jax.random.fold_in(key_list[15], 71), 0),
        "up_state_map": centred(key_list[8], (UPPERS, NX, NX), (2 * NX) ** -0.5, 0.1875, ((0, 16),)),
        "up_input_map": centred(key_list[9], (UPPERS, NX, NU), NX ** -0.5, 0.25, ((0, 16),)),
        "up_weight": jnp.clip(jnp.exp(math.log(3.0) - 2.3025851 * jax.random.uniform(key_list[10], (UPPERS,), jnp.float32) ** level_of(key_list[10], (UPPERS,), ((0, 16),), -0.2, 0.2)), 0.3, 3.0),
        "root_cov": draw_root_cov(jax.random.fold_in(key_list[15], 71), 0),
        "state_cost": jnp.clip(jnp.exp(jax.random.uniform(key_list[12], (NX,), jnp.float32, math.log(0.3), math.log(3.0))), 0.3, 3.0),
        "control_cost": jnp.clip(jnp.exp(jax.random.uniform(key_list[13], (NU,), jnp.float32, math.log(0.3), math.log(3.0))), 0.3, 3.0),
        "noise_cov": jnp.clip(jnp.exp(jax.random.uniform(key_list[14], (NX,), jnp.float32, math.log(0.05), math.log(0.5))), 0.05, 0.5),
    }


exact_mode = lax.Precision.HIGHEST

def contract(joined, applied):
    return lax.dot_general(joined.astype(jnp.float32), applied.astype(jnp.float32), (((0,), (0,)), ((), ())), preferred_element_type=jnp.float32)

def leaf_term(state_map, input_map, state_cost):
    joined = jnp.concatenate([state_map, input_map], axis=1)
    applied = (state_cost[:, None] * joined.astype(jnp.float32)).astype(jnp.bfloat16)
    return contract(joined, applied)

def node_term(value_matrix, state_map, input_map):
    joined = jnp.concatenate([state_map, input_map], axis=1)
    applied = jnp.dot(value_matrix.astype(jnp.float32), joined.astype(jnp.float32), preferred_element_type=jnp.float32).astype(jnp.bfloat16)
    return contract(joined, applied)

def riccati(combined, state_cost, control_cost):
    block_aa = combined[:NX, :NX]
    block_ba = combined[NX:, :NX]
    block_bb = combined[NX:, NX:]
    hessian = block_bb + jnp.diag(control_cost)
    factor = jnp.linalg.cholesky(hessian)
    feedback = -jax.scipy.linalg.cho_solve((factor, True), block_ba)
    value_matrix = jnp.diag(state_cost) + block_aa + jnp.dot(block_ba.T, feedback, precision=exact_mode)
    return (feedback.astype(jnp.bfloat16), value_matrix.astype(jnp.bfloat16))

def propagate(parent_cov, feedback, state_map, input_map, noise_cov):
    closed = (state_map.astype(jnp.float32) + jnp.dot(input_map.astype(jnp.float32), feedback.astype(jnp.float32), preferred_element_type=jnp.float32)).astype(jnp.bfloat16)
    moved_cov = jnp.dot(closed.astype(jnp.float32), parent_cov.astype(jnp.float32), preferred_element_type=jnp.float32).astype(jnp.bfloat16)
    spread = lax.dot_general(moved_cov.astype(jnp.float32), closed.astype(jnp.float32), (((1,), (1,)), ((), ())), preferred_element_type=jnp.float32)
    return (spread + jnp.diag(noise_cov)).astype(jnp.bfloat16)

def reference(leaf_state_map, leaf_input_map, leaf_weight, leaf_count, mid_state_map, mid_input_map, mid_weight, mid_parent, up_state_map, up_input_map, up_weight, root_cov, state_cost, control_cost, noise_cov):
    slot_ids = jnp.arange(LEAF_DEV, dtype=jnp.int32)

    def lower_node(node_inputs):
        states, controls, weights, live_count, node_state, node_input, node_weight = node_inputs
        live_weight = jnp.where(slot_ids < live_count, weights, jnp.zeros_like(weights))

        def add_leaf(running, leaf_index):
            fresh_term = leaf_term(states[leaf_index], controls[leaf_index], state_cost)
            return (running + live_weight[leaf_index] * fresh_term, None)
        child_sum, unused = lax.scan(add_leaf, jnp.zeros((NX + NU, NX + NU), jnp.float32), slot_ids)
        feedback, value_matrix = riccati(child_sum / jnp.sum(live_weight), state_cost, control_cost)
        return (feedback, value_matrix, node_weight * node_term(value_matrix, node_state, node_input))

    def row_step(carry_state, row_inputs):
        states, controls, weights, counts, node_states, node_inputs, node_weights, parents = row_inputs
        row_gains, row_values, row_terms = lax.map(lower_node, (states, controls, weights, counts, node_states, node_inputs, node_weights))
        slot_pick = (parents[:, None] == jnp.arange(S1_ROW, dtype=jnp.int32)[None, :]).astype(jnp.float32)
        slot_sums = jnp.einsum('cs,cij->sij', slot_pick, row_terms, precision=exact_mode)
        slot_weights = jnp.sum(slot_pick * node_weights[:, None], axis=0)
        return (carry_state, (row_gains, row_values, slot_sums / slot_weights[:, None, None]))
    row_inputs = (leaf_state_map.reshape(N_ROW, N_COL, LEAF_DEV, NX, NX), leaf_input_map.reshape(N_ROW, N_COL, LEAF_DEV, NX, NU), leaf_weight.astype(jnp.float32).reshape(N_ROW, N_COL, LEAF_DEV), leaf_count.reshape(N_ROW, N_COL), mid_state_map.reshape(N_ROW, N_COL, NX, NX), mid_input_map.reshape(N_ROW, N_COL, NX, NU), mid_weight.reshape(N_ROW, N_COL), mid_parent.reshape(N_ROW, N_COL))
    scan_end, row_outputs = lax.scan(row_step, jnp.zeros((), jnp.float32), row_inputs)
    mid_gain = row_outputs[0].reshape(MIDS, NU, NX)
    mid_value = row_outputs[1].reshape(MIDS, NX, NX)
    up_totals = row_outputs[2].reshape(UPPERS, NX + NU, NX + NU)

    def upper_node(node_inputs):
        node_total, node_state, node_input, node_weight = node_inputs
        feedback, value_matrix = riccati(node_total, state_cost, control_cost)
        return (feedback, value_matrix, node_weight * node_term(value_matrix, node_state, node_input))
    up_gain, up_value, up_terms = lax.map(upper_node, (up_totals, up_state_map, up_input_map, up_weight))
    root_gain, root_value = riccati(jnp.sum(up_terms, axis=0) / jnp.sum(up_weight), state_cost, control_cost)
    up_cov = lax.map(lambda node_maps: propagate(root_cov, root_gain, node_maps[0], node_maps[1], noise_cov), (up_state_map, up_input_map))
    parent_index = jnp.arange(MIDS, dtype=jnp.int32) // N_COL * S1_ROW + mid_parent

    def mid_down(node_inputs):
        parent_id, node_state, node_input = node_inputs
        return propagate(up_cov[parent_id], up_gain[parent_id], node_state, node_input, noise_cov)
    mid_cov = lax.map(mid_down, (parent_index, mid_state_map, mid_input_map))

    def leaf_down(node_inputs):
        states, controls, live_count, parent_cov, feedback = node_inputs

        def one_leaf(leaf_index):
            leaf_result = propagate(parent_cov, feedback, states[leaf_index], controls[leaf_index], noise_cov)
            return jnp.where(leaf_index < live_count, leaf_result, jnp.zeros_like(leaf_result))
        return lax.map(one_leaf, slot_ids)
    leaf_cov = lax.map(leaf_down, (leaf_state_map.reshape(MIDS, LEAF_DEV, NX, NX), leaf_input_map.reshape(MIDS, LEAF_DEV, NX, NU), leaf_count, mid_cov, mid_gain))
    leaf_cov = leaf_cov.reshape(LEAVES, NX, NX)
    return (root_gain, root_value, up_gain, up_value, up_cov, mid_gain, mid_value, mid_cov, leaf_cov)
```

```python
import functools

import jax
import jax.numpy as jnp
from jax import lax
from jax.experimental import pallas as pl
from jax.experimental.pallas import tpu as pltpu
from jax.sharding import PartitionSpec as P

NX = 512
NU = 256
H = 256
LEAF = 4
ROWS = 6 * H
BLOCKS = ((0, 0), (1, 0), (1, 1), (2, 0), (2, 1), (2, 2))
F32 = jnp.float32
BF16 = jnp.bfloat16
MESH = pl.DeviceIdType.MESH
VMEM_LIMIT = 56 * 1024 * 1024
N_CHUNK = 16
CHUNK = ROWS // N_CHUNK
N_GV = 12
GV_ROWS = NX + NU
GV_CHUNK = GV_ROWS // N_GV
PIECE = ROWS // 16
HALF = PIECE // 2
REFINE_TOL = 1e-6
MAX_REFINE = 8


def mm(a, b):
    return jnp.dot(a, b, preferred_element_type=F32)


def mm_tn(a, b):
    return lax.dot_general(a, b, (((0,), (0,)), ((), ())), preferred_element_type=F32)


def mm_nt(a, b):
    return lax.dot_general(a, b, (((1,), (1,)), ((), ())), preferred_element_type=F32)


def split(a):
    hi = a.astype(BF16)
    return hi, (a - hi.astype(F32)).astype(BF16)


def iota2(shape, dim):
    return lax.broadcasted_iota(jnp.int32, shape, dim)


def eye_mask(n):
    return iota2((n, n), 0) == iota2((n, n), 1)


def to_column(row):
    n = row.shape[1]
    parts = []
    for i in range(n // 128):
        block = jnp.broadcast_to(row[:, i * 128 : (i + 1) * 128], (128, 128))
        parts.append(jnp.sum(jnp.where(eye_mask(128), block, 0.0), axis=1, keepdims=True))
    return jnp.concatenate(parts, axis=0)


def add_diag(block, row):
    return block + jnp.where(eye_mask(block.shape[0]), row, 0.0)


def all_sum(a):
    return jnp.sum(jnp.sum(a, axis=1, keepdims=True), axis=0, keepdims=True)


def riccati(get, state_row, control_row, gain_ref, value_ref, work, feed):
    hess = add_diag(get(5), control_row)
    ba = jnp.concatenate([get(3), get(4)], axis=1)
    eye = eye_mask(H)
    upper = jnp.max(jnp.max(jnp.sum(jnp.abs(hess), axis=1, keepdims=True), axis=0, keepdims=True))
    lower = jnp.minimum(jnp.min(control_row), upper)
    mid = 0.5 * (upper + lower)
    rad = 0.5 * (upper - lower)
    den = 2.0 * mid * mid - rad * rad
    error0 = rad * rad / den
    steps = jnp.int32(0)
    for j in range(16):
        steps += (error0 > 0.1 ** (0.5**j)).astype(jnp.int32)
    h_hi, h_lo = split(hess)
    ba_hi, ba_lo = split(ba)
    work[...] = jnp.where(eye, 4.0 * mid / den, 0.0) - (2.0 / den) * hess

    def newton(_, carry):
        x = work[...]
        x_hi = x.astype(BF16)
        res = jnp.where(eye, 1.0, 0.0) - mm(h_hi, x_hi)
        work[...] = x + mm(x_hi, res.astype(BF16))
        return carry

    lax.fori_loop(0, steps, newton, 0)
    inv = work[...].astype(BF16)
    feed[...] = -mm(inv, ba_hi)

    def unconverged(state):
        count, done = state
        return jnp.logical_and(count < MAX_REFINE, done == 0)

    def refine(state):
        count, _ = state
        f = feed[...]
        f_hi, f_lo = split(f)
        res = ba + (mm(h_hi, f_hi) + (mm(h_hi, f_lo) + mm(h_lo, f_hi)))
        step = mm(inv, res.astype(BF16))
        new = f - step
        feed[...] = new
        small = jnp.sum(step * step) <= REFINE_TOL * jnp.sum(new * new)
        return count + 1, small.astype(jnp.int32)

    _, done = lax.while_loop(unconverged, refine, (jnp.int32(0), jnp.int32(0)))

    @pl.when(done == 0)
    def _():
        work[...] = hess

        def sweep(k, carry):
            a = work[...]
            row = work[pl.ds(k, 1), :]
            here = iota2((H, H), 1) == k
            col = jnp.sum(jnp.where(here, a, 0.0), axis=1, keepdims=True)
            lane_k = iota2((1, H), 1) == k
            sub_k = iota2((H, 1), 0) == k
            pivot = jnp.sum(jnp.where(lane_k, row, 0.0), axis=1, keepdims=True)
            inv_p = 1.0 / pivot
            col0 = jnp.where(sub_k, 0.0, col)
            row1 = jnp.where(lane_k, 1.0, row) * inv_p
            base = jnp.where(jnp.logical_or(here, sub_k), 0.0, a)
            work[...] = jnp.where(sub_k, row1, base - col0 * row1)
            return carry

        lax.fori_loop(0, H, sweep, 0)
        feed[...] = -jnp.dot(
            work[...], ba, preferred_element_type=F32, precision=lax.Precision.HIGHEST
        )

    f = feed[...]
    f_hi, f_lo = split(f)
    gain_ref[...] = f_hi

    def quad(i, j):
        a = slice(i * H, (i + 1) * H)
        b = slice(j * H, (j + 1) * H)
        return mm_tn(ba_hi[:, a], f_hi[:, b]) + (
            mm_tn(ba_hi[:, a], f_lo[:, b]) + mm_tn(ba_lo[:, a], f_hi[:, b])
        )

    value_ref[:H, :H] = add_diag(get(0) + quad(0, 0), state_row[:, :H]).astype(BF16)
    cross = get(1) + quad(1, 0)
    value_ref[H:, :H] = cross.astype(BF16)
    value_ref[:H, H:] = cross.T.astype(BF16)
    value_ref[H:, H:] = add_diag(get(2) + quad(1, 1), state_row[:, H:]).astype(BF16)


def node_term(value_ref, state_ref, input_ref, put):
    value = value_ref[...]
    xs = [state_ref[:, :H], state_ref[:, H:], input_ref[...]]
    ys = [mm(value, x).astype(BF16) for x in xs]
    for i, (a, b) in enumerate(BLOCKS):
        put(i, mm_tn(xs[a], ys[b]))


def propagate(cov, gain, state, inputs, noise_row):
    closed = (state.astype(F32) + mm(inputs, gain)).astype(BF16)
    moved = mm(closed, cov).astype(BF16)
    top = mm_nt(moved[:H], closed[:H])
    cross = mm_nt(moved[H:], closed[:H])
    low = mm_nt(moved[H:], closed[H:])
    return (
        add_diag(top, noise_row[:, :H]).astype(BF16),
        cross.astype(BF16),
        cross.T.astype(BF16),
        add_diag(low, noise_row[:, H:]).astype(BF16),
    )


def store_cov(ref, blocks):
    ref[:H, :H] = blocks[0]
    ref[H:, :H] = blocks[1]
    ref[:H, H:] = blocks[2]
    ref[H:, H:] = blocks[3]


def lane(row, k):
    return jnp.sum(jnp.where(iota2(row.shape, 1) == k, row, 0.0), axis=1, keepdims=True)


def lower_kernel(
    count_ref, parent_ref, midw_ref, leaf_s, leaf_u, mid_s, mid_u, leafw_ref, sc_ref, cc_ref,
    gain_ref, value_ref, own_ref, other_ref, tile_ref,
    ls, lu, ms, mu, total, work, feed, sems,
):
    copies = []
    for c in range(LEAF):
        copies.append(pltpu.make_async_copy(leaf_s.at[c], ls.at[pl.ds(c * NX, NX)], sems.at[2 * c]))
        copies.append(pltpu.make_async_copy(leaf_u.at[c], lu.at[pl.ds(c * NX, NX)], sems.at[2 * c + 1]))
    copies.append(pltpu.make_async_copy(mid_s.at[0], ms, sems.at[2 * LEAF]))
    copies.append(pltpu.make_async_copy(mid_u.at[0], mu, sems.at[2 * LEAF + 1]))
    for copy in copies:
        copy.start()
    live = count_ref[0]
    weights = leafw_ref[...].astype(F32)
    weights = jnp.where(iota2(weights.shape, 1) < live, weights, 0.0)
    weights = weights / jnp.sum(weights, axis=1, keepdims=True)
    cost = to_column(sc_ref[...])
    for c in range(LEAF):
        copies[2 * c].wait()
        copies[2 * c + 1].wait()
        scale = cost * lane(weights, c)
        rows = slice(c * NX, (c + 1) * NX)
        xs = [ls[rows, :H], ls[rows, H:], lu[rows, :]]
        ss = [(scale * x.astype(F32)).astype(BF16) for x in xs]
        for i, (a, b) in enumerate(BLOCKS):
            part = mm_tn(xs[a], ss[b])
            if c == 0:
                total[i] = part
            else:
                total[i] += part
    riccati(lambda i: total[i], sc_ref[...], cc_ref[...], gain_ref, value_ref, work, feed)
    copies[2 * LEAF].wait()
    copies[2 * LEAF + 1].wait()
    weight = midw_ref[0]
    parent = parent_ref[0]
    core = lax.rem(lax.axis_index("col"), 2)
    w_own = jnp.where(parent == core, weight, 0.0)
    w_other = jnp.where(parent == core, 0.0, weight)

    def put(i, block):
        own_ref[i * H : (i + 1) * H, :] = (w_own * block).astype(BF16)
        other_ref[i * H : (i + 1) * H, :] = (w_other * block).astype(BF16)

    node_term(value_ref, ms, mu, put)
    tile_ref[...] = jnp.where(iota2((8, 128), 0) == parent, weight, 0.0)


def lower(count, parent, midw, leaf_s, leaf_u, mid_s, mid_u, leafw, sc, cc):
    smem = pl.BlockSpec(memory_space=pltpu.SMEM)
    vmem = pl.BlockSpec(memory_space=pltpu.VMEM)
    hbm = pl.BlockSpec(memory_space=pl.ANY)
    return pl.pallas_call(
        lower_kernel,
        out_shape=(
            jax.ShapeDtypeStruct((NU, NX), BF16),
            jax.ShapeDtypeStruct((NX, NX), BF16),
            jax.ShapeDtypeStruct((ROWS, H), BF16),
            jax.ShapeDtypeStruct((ROWS, H), BF16),
            jax.ShapeDtypeStruct((8, 128), F32),
        ),
        in_specs=[smem] * 3 + [hbm] * 4 + [vmem] * 3,
        out_specs=(vmem,) * 5,
        scratch_shapes=[
            pltpu.VMEM((LEAF * NX, NX), BF16),
            pltpu.VMEM((LEAF * NX, NU), BF16),
            pltpu.VMEM((NX, NX), BF16),
            pltpu.VMEM((NX, NU), BF16),
            pltpu.VMEM((6, H, H), F32),
            pltpu.VMEM((H, H), F32),
            pltpu.VMEM((NU, NX), F32),
            pltpu.SemaphoreType.DMA((2 * LEAF + 2,)),
        ],
        compiler_params=pltpu.CompilerParams(vmem_limit_bytes=VMEM_LIMIT),
        name="lower_nodes",
    )(count, parent, midw, leaf_s, leaf_u, mid_s, mid_u, leafw, sc, cc)


def gather_kernel(
    own_ref, other_ref, tile_ref, total_ref, tiles_ref,
    sib_buf, in_buf, out_buf, sib_send, sib_recv, send_sem, recv_sem, tile_send, tile_recv,
):
    row = lax.axis_index("row")
    col = lax.axis_index("col")
    z = col // 2
    core = lax.rem(col, 2)
    sibling = col + 1 - 2 * core
    dist = lax.rem(z + 8 - 4 * core, 8)
    is_target = dist == 0
    down = jnp.logical_and(dist >= 1, dist <= 4)
    next_z = jnp.where(down, lax.rem(z + 7, 8), lax.rem(z + 1, 8))
    next_col = 2 * next_z + core
    side = jnp.where(dist == 7, 1, 0)
    has_up = jnp.logical_and(dist != 4, dist != 5)

    barrier = pltpu.get_barrier_semaphore()

    def greet(k, carry):
        pl.semaphore_signal(
            barrier, inc=1, device_id=(row, lax.rem(col + k, 16)), device_id_type=MESH
        )
        return carry

    lax.fori_loop(1, 16, greet, 0)
    pl.semaphore_wait(barrier, 15)

    def sib_copy(c):
        rows = pl.ds(pl.multiple_of(c * CHUNK, 16), CHUNK)
        return pltpu.make_async_remote_copy(
            src_ref=other_ref.at[rows],
            dst_ref=sib_buf.at[rows],
            send_sem=sib_send.at[c],
            recv_sem=sib_recv.at[c],
            device_id=(row, sibling),
            device_id_type=MESH,
        )

    def chain_copy(c, to_side):
        rows = pl.ds(pl.multiple_of(c * CHUNK, 16), CHUNK)
        return pltpu.make_async_remote_copy(
            src_ref=out_buf.at[rows],
            dst_ref=in_buf.at[to_side, rows],
            send_sem=send_sem.at[c],
            recv_sem=recv_sem.at[to_side, c],
            device_id=(row, next_col),
            device_id_type=MESH,
        )

    def tile_copy(slot):
        return pltpu.make_async_remote_copy(
            src_ref=tile_ref,
            dst_ref=tiles_ref.at[col],
            send_sem=tile_send.at[slot],
            recv_sem=tile_recv.at[col],
            device_id=(row, 9 * slot),
            device_id_type=MESH,
        )

    def tile_arrival(source):
        return pltpu.make_async_remote_copy(
            src_ref=tile_ref,
            dst_ref=tiles_ref.at[source],
            send_sem=tile_send.at[0],
            recv_sem=tile_recv.at[source],
            device_id=(row, sibling),
            device_id_type=MESH,
        )

    def start_sib(c, carry):
        sib_copy(c).start()
        return carry

    lax.fori_loop(0, N_CHUNK, start_sib, 0)
    for slot in range(2):

        @pl.when(col != 9 * slot)
        def _():
            tile_copy(slot).start()

    def step(c, carry):
        rows = pl.ds(pl.multiple_of(c * CHUNK, 16), CHUNK)
        sib_copy(c).wait_recv()
        part = own_ref[rows, :].astype(F32) + sib_buf[rows, :].astype(F32)

        @pl.when(jnp.logical_not(has_up))
        def _():
            out_buf[rows, :] = part.astype(BF16)
            chain_copy(c, side).start()

        @pl.when(has_up)
        def _():
            chain_copy(c, 0).wait_recv()
            more = part + in_buf[0, rows, :].astype(F32)

            @pl.when(is_target)
            def _():
                chain_copy(c, 1).wait_recv()
                total_ref[rows, :] = more + in_buf[1, rows, :].astype(F32)

            @pl.when(jnp.logical_not(is_target))
            def _():
                out_buf[rows, :] = more.astype(BF16)
                chain_copy(c, side).start()

        return carry

    lax.fori_loop(0, N_CHUNK, step, 0)

    def drain(c, carry):
        sib_copy(c).wait_send()

        @pl.when(jnp.logical_not(is_target))
        def _():
            chain_copy(c, side).wait_send()

        return carry

    lax.fori_loop(0, N_CHUNK, drain, 0)
    for slot in range(2):

        @pl.when(col != 9 * slot)
        def _():
            tile_copy(slot).wait_send()

    @pl.when(is_target)
    def _():
        def arrive(k, carry):
            tile_arrival(lax.rem(col + k, 16)).wait_recv()
            return carry

        lax.fori_loop(1, 16, arrive, 0)
        tiles_ref[pl.ds(col, 1)] = tile_ref[...][None]


def gather(own, other, tile):
    vmem = pl.BlockSpec(memory_space=pltpu.VMEM)
    return pl.pallas_call(
        gather_kernel,
        out_shape=(
            jax.ShapeDtypeStruct((ROWS, H), F32),
            jax.ShapeDtypeStruct((16, 8, 128), F32),
        ),
        in_specs=[vmem] * 3,
        out_specs=(vmem,) * 2,
        scratch_shapes=[
            pltpu.VMEM((ROWS, H), BF16),
            pltpu.VMEM((2, ROWS, H), BF16),
            pltpu.VMEM((ROWS, H), BF16),
            pltpu.SemaphoreType.DMA((N_CHUNK,)),
            pltpu.SemaphoreType.DMA((N_CHUNK,)),
            pltpu.SemaphoreType.DMA((N_CHUNK,)),
            pltpu.SemaphoreType.DMA((2, N_CHUNK)),
            pltpu.SemaphoreType.DMA((2,)),
            pltpu.SemaphoreType.DMA((16,)),
        ],
        compiler_params=pltpu.CompilerParams(
            collective_id=0, has_side_effects=True, vmem_limit_bytes=VMEM_LIMIT
        ),
        name="group_sum",
    )(own, other, tile)


def upper_kernel(
    upw_ref, total_ref, tiles_ref, up_s, up_u, sc_ref, cc_ref,
    gv_ref, term_ref, wtile_ref,
    us, uu, blocks, work, feed, sems,
):
    col = lax.axis_index("col")
    core = lax.rem(col, 2)
    wtile_ref[...] = jnp.full((8, 128), upw_ref[0] + upw_ref[1], F32)

    @pl.when(col == 9 * core)
    def _():
        copies = [
            pltpu.make_async_copy(up_s.at[core], us, sems.at[0]),
            pltpu.make_async_copy(up_u.at[core], uu, sems.at[1]),
        ]
        for copy in copies:
            copy.start()
        sums = jnp.sum(tiles_ref[...], axis=0)
        weight = jnp.sum(jnp.where(iota2((8, 128), 0) == core, sums, 0.0), axis=0, keepdims=True)
        scale = 1.0 / weight[:, :1]
        for i in range(6):
            blocks[i] = total_ref[i * H : (i + 1) * H, :] * scale
        gain_ref = gv_ref.at[pl.ds(0, NU)]
        value_ref = gv_ref.at[pl.ds(NU, NX)]
        riccati(lambda i: blocks[i], sc_ref[...], cc_ref[...], gain_ref, value_ref, work, feed)
        for copy in copies:
            copy.wait()
        up_weight = upw_ref[core]

        def put(i, block):
            term_ref[i * H : (i + 1) * H, :] = (up_weight * block).astype(BF16)

        node_term(value_ref, us, uu, put)


def upper(upw, total, tiles, up_s, up_u, sc, cc):
    smem = pl.BlockSpec(memory_space=pltpu.SMEM)
    vmem = pl.BlockSpec(memory_space=pltpu.VMEM)
    hbm = pl.BlockSpec(memory_space=pl.ANY)
    return pl.pallas_call(
        upper_kernel,
        out_shape=(
            jax.ShapeDtypeStruct((GV_ROWS, NX), BF16),
            jax.ShapeDtypeStruct((ROWS, H), BF16),
            jax.ShapeDtypeStruct((8, 128), F32),
        ),
        in_specs=[smem, vmem, vmem, hbm, hbm, vmem, vmem],
        out_specs=(vmem,) * 3,
        scratch_shapes=[
            pltpu.VMEM((NX, NX), BF16),
            pltpu.VMEM((NX, NU), BF16),
            pltpu.VMEM((6, H, H), F32),
            pltpu.VMEM((H, H), F32),
            pltpu.VMEM((NU, NX), F32),
            pltpu.SemaphoreType.DMA((2,)),
        ],
        compiler_params=pltpu.CompilerParams(vmem_limit_bytes=VMEM_LIMIT),
        name="upper_nodes",
    )(upw, total, tiles, up_s, up_u, sc, cc)


def root_kernel(
    gv_ref, term_ref, wtile_ref, gvs_ref, total_ref, wtiles_ref,
    in_buf, piece_buf, pair_buf,
    w_send, w_recv, a_send, a_recv, b_send, b_recv, c_send, c_recv, s_send, s_recv,
    g_send, g_recv, gs_send, gs_recv,
):
    row = lax.axis_index("row")
    col = lax.axis_index("col")
    z = col // 2
    core = lax.rem(col, 2)
    sibling = col + 1 - 2 * core
    dist = lax.rem(z + 8 - 4 * core, 8)
    is_target = dist == 0
    barrier = pltpu.get_barrier_semaphore()

    def greet(k, carry):
        pl.semaphore_signal(
            barrier, inc=1, device_id=(row, lax.rem(col + k, 16)), device_id_type=MESH
        )
        pl.semaphore_signal(
            barrier, inc=1, device_id=(lax.rem(row + k, 16), col), device_id_type=MESH
        )
        return carry

    lax.fori_loop(1, 16, greet, 0)
    pl.semaphore_wait(barrier, 30)

    def a_copy(to_row, at):
        return pltpu.make_async_remote_copy(
            src_ref=term_ref.at[pl.ds(pl.multiple_of(to_row * PIECE, 16), PIECE)],
            dst_ref=in_buf.at[at],
            send_sem=a_send.at[to_row],
            recv_sem=a_recv.at[at],
            device_id=(to_row, col),
            device_id_type=MESH,
        )

    def b_copy(to_col, slot):
        half = lax.rem(to_col, 2)
        return pltpu.make_async_remote_copy(
            src_ref=piece_buf.at[half],
            dst_ref=pair_buf.at[slot],
            send_sem=b_send.at[to_col],
            recv_sem=b_recv.at[slot],
            device_id=(row, to_col),
            device_id_type=MESH,
        )

    def c_copy(to_row, at):
        return pltpu.make_async_remote_copy(
            src_ref=total_ref.at[at, core],
            dst_ref=total_ref.at[at, core],
            send_sem=c_send.at[to_row],
            recv_sem=c_recv.at[at],
            device_id=(to_row, col),
            device_id_type=MESH,
        )

    def s_copy(at, half):
        return pltpu.make_async_remote_copy(
            src_ref=total_ref.at[at, half],
            dst_ref=total_ref.at[at, half],
            send_sem=s_send.at[at],
            recv_sem=s_recv.at[at],
            device_id=(row, sibling),
            device_id_type=MESH,
        )

    def w_copy(to_row, at):
        return pltpu.make_async_remote_copy(
            src_ref=wtile_ref,
            dst_ref=wtiles_ref.at[at],
            send_sem=w_send.at[to_row],
            recv_sem=w_recv.at[at],
            device_id=(to_row, col),
            device_id_type=MESH,
        )

    def g_rows(c):
        return pl.ds(pl.multiple_of(c * GV_CHUNK, 16), GV_CHUNK)

    def g_copy(c, slot, to_col, lane_id):
        return pltpu.make_async_remote_copy(
            src_ref=gvs_ref.at[slot, g_rows(c)],
            dst_ref=gvs_ref.at[slot, g_rows(c)],
            send_sem=g_send.at[lane_id, c],
            recv_sem=g_recv.at[c],
            device_id=(row, to_col),
            device_id_type=MESH,
        )

    def gs_copy(c, slot):
        return pltpu.make_async_remote_copy(
            src_ref=gvs_ref.at[slot, g_rows(c)],
            dst_ref=gvs_ref.at[slot, g_rows(c)],
            send_sem=gs_send.at[c],
            recv_sem=gs_recv.at[c],
            device_id=(row, sibling),
            device_id_type=MESH,
        )

    def peers(body):
        def one(k, carry):
            body(lax.rem(row + k, 16))
            return carry

        lax.fori_loop(1, 16, one, 0)

    def columns(body):
        def one(k, carry):
            body(lax.rem(col + k, 16))
            return carry

        lax.fori_loop(1, 16, one, 0)

    def gv_chunks(body):
        def one(c, carry):
            body(c)
            return carry

        lax.fori_loop(0, N_GV, one, 0)

    up_col = 2 * lax.rem(z + 1, 8) + core
    down_col = 2 * lax.rem(z + 7, 8) + core
    to_up = dist <= 3
    to_down = jnp.logical_or(dist == 0, dist >= 6)

    def forward(c):
        @pl.when(to_up)
        def _():
            g_copy(c, core, up_col, 0).start()

        @pl.when(to_down)
        def _():
            g_copy(c, core, down_col, 1).start()

        gs_copy(c, core).start()

    peers(lambda p: w_copy(p, row).start())

    @pl.when(is_target)
    def _():
        peers(lambda p: a_copy(p, row).start())
        gvs_ref[pl.ds(core, 1)] = gv_ref[...][None]
        gv_chunks(forward)
        acc = term_ref[pl.ds(pl.multiple_of(row * PIECE, 16), PIECE), :].astype(F32)

        def add(k, acc):
            source = lax.rem(row + k, 16)
            a_copy(source, source).wait_recv()
            return acc + in_buf[source].astype(F32)

        acc = lax.fori_loop(1, 16, add, acc)
        piece = acc.astype(BF16)
        piece_buf[0] = piece[:HALF]
        piece_buf[1] = piece[HALF:]
        columns(lambda p: b_copy(p, core).start())
        pair_buf[pl.ds(core, 1)] = piece_buf[pl.ds(core, 1)]
        b_copy(col, 1 - core).wait_recv()

    @pl.when(jnp.logical_not(is_target))
    def _():
        b_copy(col, 0).wait_recv()
        b_copy(col, 1).wait_recv()

    pair = pair_buf[0].astype(F32) + pair_buf[1].astype(F32)
    total_ref[pl.ds(row, 1), pl.ds(core, 1)] = pair.astype(BF16)[None, None]
    peers(lambda p: c_copy(p, row).start())
    s_copy(row, core).start()

    @pl.when(jnp.logical_not(is_target))
    def _():
        def relay(c):
            g_copy(c, core, up_col, 0).wait_recv()
            forward(c)

        gv_chunks(relay)

    def relay_piece(p):
        c_copy(p, p).wait_recv()
        s_copy(p, core).start()

    peers(relay_piece)

    def finish(at, carry):
        s_copy(at, 1 - core).wait_recv()
        s_copy(at, core).wait_send()
        return carry

    lax.fori_loop(0, 16, finish, 0)

    def finish_peer(p):
        c_copy(p, row).wait_send()
        w_copy(p, row).wait_send()
        w_copy(p, p).wait_recv()

    peers(finish_peer)
    wtiles_ref[pl.ds(row, 1)] = wtile_ref[...][None]

    @pl.when(is_target)
    def _():
        peers(lambda p: a_copy(p, row).wait_send())
        columns(lambda p: b_copy(p, core).wait_send())

    def finish_gv(c):
        gs_copy(c, 1 - core).wait_recv()
        gs_copy(c, core).wait_send()

        @pl.when(to_up)
        def _():
            g_copy(c, core, up_col, 0).wait_send()

        @pl.when(to_down)
        def _():
            g_copy(c, core, down_col, 1).wait_send()

    gv_chunks(finish_gv)


def root_sum(gv, term, wtile):
    vmem = pl.BlockSpec(memory_space=pltpu.VMEM)
    dma = pltpu.SemaphoreType.DMA
    return pl.pallas_call(
        root_kernel,
        out_shape=(
            jax.ShapeDtypeStruct((2, GV_ROWS, NX), BF16),
            jax.ShapeDtypeStruct((16, 2, HALF, H), BF16),
            jax.ShapeDtypeStruct((16, 8, 128), F32),
        ),
        in_specs=[vmem] * 3,
        out_specs=(vmem,) * 3,
        scratch_shapes=[
            pltpu.VMEM((16, PIECE, H), BF16),
            pltpu.VMEM((2, HALF, H), BF16),
            pltpu.VMEM((2, HALF, H), BF16),
            dma((16,)), dma((16,)),
            dma((16,)), dma((16,)),
            dma((16,)), dma((2,)),
            dma((16,)), dma((16,)),
            dma((16,)), dma((16,)),
            dma((2, N_GV)), dma((N_GV,)),
            dma((N_GV,)), dma((N_GV,)),
        ],
        compiler_params=pltpu.CompilerParams(
            collective_id=1, has_side_effects=True, vmem_limit_bytes=VMEM_LIMIT
        ),
        name="root_sum",
    )(gv, term, wtile)


def down_kernel(
    count_ref, parent_ref, gvs_ref, total_ref, wtiles_ref, mid_gain_ref, root_cov_ref,
    up_s, up_u, mid_s, mid_u, leaf_s, leaf_u, sc_ref, cc_ref, nc_ref,
    root_gain_ref, root_value_ref, up_gain_out, up_value_out, up_cov_ref, mid_cov_ref, leaf_cov_out,
    us, uu, ms, mu, ls, lu, lcov, blocks, work, feed, sems, out_sems,
):
    copies = [
        pltpu.make_async_copy(up_s, us, sems.at[0]),
        pltpu.make_async_copy(up_u, uu, sems.at[1]),
        pltpu.make_async_copy(mid_s.at[0], ms, sems.at[2]),
        pltpu.make_async_copy(mid_u.at[0], mu, sems.at[3]),
        pltpu.make_async_copy(leaf_s, ls, sems.at[4]),
        pltpu.make_async_copy(leaf_u, lu, sems.at[5]),
    ]
    for copy in copies:
        copy.start()
    outs = []
    for s in range(2):
        outs.append(
            pltpu.make_async_copy(gvs_ref.at[s, pl.ds(0, NU)], up_gain_out.at[s], out_sems.at[2 * s])
        )
        outs.append(
            pltpu.make_async_copy(gvs_ref.at[s, pl.ds(NU, NX)], up_value_out.at[s], out_sems.at[2 * s + 1])
        )
    for copy in outs:
        copy.start()
    weight = jnp.sum(wtiles_ref[...], axis=0)
    scale = 1.0 / weight[:1, :1]
    for i in range(6):
        blocks[i] = total_ref[i * H : (i + 1) * H, :].astype(F32) * scale
    riccati(
        lambda i: blocks[i], sc_ref[...], cc_ref[...], root_gain_ref, root_value_ref, work, feed
    )
    noise = nc_ref[...]
    copies[0].wait()
    copies[1].wait()
    root_gain = root_gain_ref[...]
    root_cov = root_cov_ref[...]
    for s in range(2):
        store_cov(up_cov_ref.at[s], propagate(root_cov, root_gain, us[s], uu[s], noise))
    copies[2].wait()
    copies[3].wait()
    parent = parent_ref[0]
    store_cov(
        mid_cov_ref,
        propagate(up_cov_ref[parent], gvs_ref[parent, :NU, :], ms[...], mu[...], noise),
    )
    copies[4].wait()
    copies[5].wait()
    live = count_ref[0]
    mid_cov = mid_cov_ref[...]
    mid_gain = mid_gain_ref[...]
    for c in range(LEAF):
        keep = c < live
        result = propagate(mid_cov, mid_gain, ls[c], lu[c], noise)
        store_cov(lcov.at[c], [jnp.where(keep, block, jnp.zeros_like(block)) for block in result])
        out = pltpu.make_async_copy(lcov.at[c], leaf_cov_out.at[c], out_sems.at[4 + c])
        out.start()
        outs.append(out)
    for out in outs:
        out.wait()


def down(count, parent, gvs, total, wtiles, mid_gain, root_cov, up_s, up_u, mid_s, mid_u, leaf_s, leaf_u, sc, cc, nc):
    smem = pl.BlockSpec(memory_space=pltpu.SMEM)
    vmem = pl.BlockSpec(memory_space=pltpu.VMEM)
    hbm = pl.BlockSpec(memory_space=pl.ANY)
    return pl.pallas_call(
        down_kernel,
        out_shape=(
            jax.ShapeDtypeStruct((NU, NX), BF16),
            jax.ShapeDtypeStruct((NX, NX), BF16),
            jax.ShapeDtypeStruct((2, NU, NX), BF16),
            jax.ShapeDtypeStruct((2, NX, NX), BF16),
            jax.ShapeDtypeStruct((2, NX, NX), BF16),
            jax.ShapeDtypeStruct((NX, NX), BF16),
            jax.ShapeDtypeStruct((LEAF, NX, NX), BF16),
        ),
        in_specs=[smem, smem] + [vmem] * 5 + [hbm] * 6 + [vmem] * 3,
        out_specs=(vmem, vmem, hbm, hbm, vmem, vmem, hbm),
        scratch_shapes=[
            pltpu.VMEM((2, NX, NX), BF16),
            pltpu.VMEM((2, NX, NU), BF16),
            pltpu.VMEM((NX, NX), BF16),
            pltpu.VMEM((NX, NU), BF16),
            pltpu.VMEM((LEAF, NX, NX), BF16),
            pltpu.VMEM((LEAF, NX, NU), BF16),
            pltpu.VMEM((LEAF, NX, NX), BF16),
            pltpu.VMEM((6, H, H), F32),
            pltpu.VMEM((H, H), F32),
            pltpu.VMEM((NU, NX), F32),
            pltpu.SemaphoreType.DMA((6,)),
            pltpu.SemaphoreType.DMA((8,)),
        ],
        compiler_params=pltpu.CompilerParams(vmem_limit_bytes=VMEM_LIMIT),
        name="down_sweep",
    )(count, parent, gvs, total, wtiles, mid_gain, root_cov, up_s, up_u, mid_s, mid_u, leaf_s, leaf_u, sc, cc, nc)


def local(
    leaf_state_map,
    leaf_input_map,
    leaf_weight,
    leaf_count,
    mid_state_map,
    mid_input_map,
    mid_weight,
    mid_parent,
    up_state_map,
    up_input_map,
    up_weight,
    root_cov,
    state_cost,
    control_cost,
    noise_cov,
):
    sc = state_cost.reshape(1, NX)
    cc = control_cost.reshape(1, NU)
    nc = noise_cov.reshape(1, NX)
    mid_gain, mid_value, own, other, tile = lower(
        leaf_count, mid_parent, mid_weight, leaf_state_map, leaf_input_map,
        mid_state_map, mid_input_map, leaf_weight.reshape(1, LEAF), sc, cc,
    )
    total, tiles = gather(own, other, tile)
    gv, term, wtile = upper(up_weight, total, tiles, up_state_map, up_input_map, sc, cc)
    gvs, root_total, wtiles = root_sum(gv, term, wtile)
    root_gain, root_value, up_gain, up_value, up_cov, mid_cov, leaf_cov = down(
        leaf_count, mid_parent, gvs, root_total.reshape(ROWS, H), wtiles, mid_gain, root_cov,
        up_state_map, up_input_map, mid_state_map, mid_input_map, leaf_state_map, leaf_input_map,
        sc, cc, nc,
    )
    return (
        root_gain,
        root_value,
        up_gain,
        up_value,
        up_cov,
        mid_gain[None],
        mid_value[None],
        mid_cov[None],
        leaf_cov,
    )


def solution(mesh):
    both = P(("row", "col"))
    return jax.shard_map(
        local,
        mesh=mesh,
        in_specs=(
            both, both, both, both, both, both, both, both,
            P("row"), P("row"), P("row"), P(), P(), P(), P(),
        ),
        out_specs=(P(), P(), P("row"), P("row"), P("row"), both, both, both, both),
        check_vma=False,
    )
```

```python
import functools

import jax
import jax.numpy as jnp
from jax import lax
from jax.experimental import pallas as pl
from jax.experimental.pallas import tpu as pltpu
from jax.sharding import PartitionSpec as P

NX = 512
NU = 256
H = 256
LEAF = 4
ROWS = 6 * H
BLOCKS = ((0, 0), (1, 0), (1, 1), (2, 0), (2, 1), (2, 2))
F32 = jnp.float32
BF16 = jnp.bfloat16
MESH = pl.DeviceIdType.MESH
VMEM_LIMIT = 24 * 1024 * 1024
N_CHUNK = 24
CHUNK = ROWS // N_CHUNK
N_GV = 12
GV_ROWS = NX + NU
GV_CHUNK = GV_ROWS // N_GV
PIECE = ROWS // 16
HALF = PIECE // 2
ERROR_TOL = 1e-4
MAX_CONTRACTION = 0.25
MAX_RATIO = 256.0
MAX_REFINE = 8


def mm(a, b):
    return jnp.dot(a, b, preferred_element_type=F32)


def mm_tn(a, b):
    return lax.dot_general(a, b, (((0,), (0,)), ((), ())), preferred_element_type=F32)


def mm_nt(a, b):
    return lax.dot_general(a, b, (((1,), (1,)), ((), ())), preferred_element_type=F32)


def split(a):
    hi = a.astype(BF16)
    return hi, (a - hi.astype(F32)).astype(BF16)


def iota2(shape, dim):
    return lax.broadcasted_iota(jnp.int32, shape, dim)


def eye_mask(n):
    return iota2((n, n), 0) == iota2((n, n), 1)


def to_column(row):
    n = row.shape[1]
    parts = []
    for i in range(n // 128):
        block = jnp.broadcast_to(row[:, i * 128 : (i + 1) * 128], (128, 128))
        parts.append(jnp.sum(jnp.where(eye_mask(128), block, 0.0), axis=1, keepdims=True))
    return jnp.concatenate(parts, axis=0)


def add_diag(block, row):
    return block + jnp.where(eye_mask(block.shape[0]), row, 0.0)


def all_sum(a):
    return jnp.sum(jnp.sum(a, axis=1, keepdims=True), axis=0, keepdims=True)


def riccati(get, state_row, control_row, gain_ref, value_ref, work, feed):
    hess = add_diag(get(5), control_row)
    ba = jnp.concatenate([get(3), get(4)], axis=1)
    eye = eye_mask(H)
    upper = jnp.max(jnp.max(jnp.sum(jnp.abs(hess), axis=1, keepdims=True), axis=0, keepdims=True))
    lower = jnp.minimum(jnp.min(control_row), upper)
    mid = 0.5 * (upper + lower)
    rad = 0.5 * (upper - lower)
    den = 2.0 * mid * mid - rad * rad
    error0 = rad * rad / den
    steps = jnp.int32(0)
    for j in range(16):
        steps += (error0 > 0.1 ** (0.5**j)).astype(jnp.int32)
    h_hi, h_lo = split(hess)
    ba_hi, ba_lo = split(ba)
    work[...] = jnp.where(eye, 4.0 * mid / den, 0.0) - (2.0 / den) * hess

    def newton(_, carry):
        x_hi = work[...].astype(BF16)
        res = jnp.where(eye, 1.0, 0.0) - mm(h_hi, x_hi)
        work[...] = x_hi.astype(F32) + mm(x_hi, res.astype(BF16))
        return carry

    lax.fori_loop(0, steps, newton, 0)
    x_hi = work[...].astype(BF16)
    res = (jnp.where(eye, 1.0, 0.0) - mm(h_hi, x_hi)) - mm(h_lo, x_hi)
    inv, inv_lo = split(x_hi.astype(F32) + mm(x_hi, res.astype(BF16)))
    feed[...] = -(mm(inv, ba_hi) + (mm(inv, ba_lo) + mm(inv_lo, ba_hi)))

    def unconverged(state):
        count, done, _ = state
        return jnp.logical_and(count < MAX_REFINE, done == 0)

    def refine(state):
        count, _, last = state
        f = feed[...]
        f_hi, f_lo = split(f)
        res = ba + (mm(h_hi, f_hi) + (mm(h_hi, f_lo) + mm(h_lo, f_hi)))
        step = mm(inv, res.astype(BF16))
        new = f - step
        feed[...] = new
        size = jnp.sum(step * step)
        norm = jnp.sum(new * new)
        last = jnp.where(count == 0, norm, last)
        small = jnp.logical_and(
            size <= MAX_CONTRACTION**2 * last, size * size <= ERROR_TOL**2 * norm * last
        )
        return count + 1, small.astype(jnp.int32), size

    first = (upper > MAX_RATIO * lower).astype(jnp.int32) * MAX_REFINE
    _, done, _ = lax.while_loop(unconverged, refine, (first, jnp.int32(0), jnp.float32(0.0)))

    @pl.when(done == 0)
    def _():
        work[...] = hess

        def sweep(k, carry):
            a = work[...]
            row = work[pl.ds(k, 1), :]
            here = iota2((H, H), 1) == k
            col = jnp.sum(jnp.where(here, a, 0.0), axis=1, keepdims=True)
            lane_k = iota2((1, H), 1) == k
            sub_k = iota2((H, 1), 0) == k
            pivot = jnp.sum(jnp.where(lane_k, row, 0.0), axis=1, keepdims=True)
            inv_p = 1.0 / pivot
            col0 = jnp.where(sub_k, 0.0, col)
            row1 = jnp.where(lane_k, 1.0, row) * inv_p
            base = jnp.where(jnp.logical_or(here, sub_k), 0.0, a)
            work[...] = jnp.where(sub_k, row1, base - col0 * row1)
            return carry

        lax.fori_loop(0, H, sweep, 0)
        feed[...] = -jnp.dot(
            work[...], ba, preferred_element_type=F32, precision=lax.Precision.HIGHEST
        )

    f = feed[...]
    f_hi, f_lo = split(f)
    gain_ref[...] = f_hi

    def quad(i, j):
        a = slice(i * H, (i + 1) * H)
        b = slice(j * H, (j + 1) * H)
        return mm_tn(ba_hi[:, a], f_hi[:, b]) + (
            mm_tn(ba_hi[:, a], f_lo[:, b]) + mm_tn(ba_lo[:, a], f_hi[:, b])
        )

    value_ref[:H, :H] = add_diag(get(0) + quad(0, 0), state_row[:, :H]).astype(BF16)
    cross = get(1) + quad(1, 0)
    value_ref[H:, :H] = cross.astype(BF16)
    value_ref[:H, H:] = cross.T.astype(BF16)
    value_ref[H:, H:] = add_diag(get(2) + quad(1, 1), state_row[:, H:]).astype(BF16)


def node_term(value_ref, state_ref, input_ref, put):
    value = value_ref[...]
    xs = [state_ref[:, :H], state_ref[:, H:], input_ref[...]]
    ys = [mm(value, x).astype(BF16) for x in xs]
    for i, (a, b) in enumerate(BLOCKS):
        put(i, mm_tn(xs[a], ys[b]))


def propagate(cov, gain, state, inputs, noise_row):
    closed = (state.astype(F32) + mm(inputs, gain)).astype(BF16)
    moved = mm(closed, cov).astype(BF16)
    top = mm_nt(moved[:H], closed[:H])
    cross = mm_nt(moved[H:], closed[:H])
    low = mm_nt(moved[H:], closed[H:])
    return (
        add_diag(top, noise_row[:, :H]).astype(BF16),
        cross.astype(BF16),
        cross.T.astype(BF16),
        add_diag(low, noise_row[:, H:]).astype(BF16),
    )


def store_cov(ref, blocks):
    ref[:H, :H] = blocks[0]
    ref[H:, :H] = blocks[1]
    ref[:H, H:] = blocks[2]
    ref[H:, H:] = blocks[3]


def lane(row, k):
    return jnp.sum(jnp.where(iota2(row.shape, 1) == k, row, 0.0), axis=1, keepdims=True)


def lower_kernel(
    count_ref, leaf_s, leaf_u, leafw_in, sc_in, cc_in,
    gain_ref, value_ref,
    ls, lu, leafw_ref, sc_ref, cc_ref, total, work, feed, sems,
):
    copies = []
    small = []
    for i, (src, dst) in enumerate(((leafw_in, leafw_ref), (sc_in, sc_ref), (cc_in, cc_ref))):
        small.append(pltpu.make_async_copy(src, dst, sems.at[2 * LEAF + i]))
        small[-1].start()
    for c in range(LEAF):
        copies.append(pltpu.make_async_copy(leaf_s.at[c], ls.at[pl.ds(c * NX, NX)], sems.at[2 * c]))
        copies.append(pltpu.make_async_copy(leaf_u.at[c], lu.at[pl.ds(c * NX, NX)], sems.at[2 * c + 1]))
    for copy in copies:
        copy.start()
    for copy in small:
        copy.wait()
    live = count_ref[0]
    weights = leafw_ref[...].astype(F32)
    weights = jnp.where(iota2(weights.shape, 1) < live, weights, 0.0)
    weights = weights / jnp.sum(weights, axis=1, keepdims=True)
    cost = to_column(sc_ref[...])
    for c in range(LEAF):
        copies[2 * c].wait()
        copies[2 * c + 1].wait()
        scale = cost * lane(weights, c)
        rows = slice(c * NX, (c + 1) * NX)
        xs = [ls[rows, :H], ls[rows, H:], lu[rows, :]]
        ss = [(scale * x.astype(F32)).astype(BF16) for x in xs]
        for i, (a, b) in enumerate(BLOCKS):
            part = mm_tn(xs[a], ss[b])
            if c == 0:
                total[i] = part
            else:
                total[i] += part
    riccati(lambda i: total[i], sc_ref[...], cc_ref[...], gain_ref, value_ref, work, feed)


def lower(count, leaf_s, leaf_u, leafw, sc, cc):
    smem = pl.BlockSpec(memory_space=pltpu.SMEM)
    vmem = pl.BlockSpec(memory_space=pltpu.VMEM)
    hbm = pl.BlockSpec(memory_space=pltpu.HBM)
    leaf_s, leaf_u, leafw, sc, cc = [
        pltpu.with_memory_space_constraint(a, pltpu.HBM) for a in (leaf_s, leaf_u, leafw, sc, cc)
    ]
    return pl.pallas_call(
        lower_kernel,
        out_shape=(
            jax.ShapeDtypeStruct((NU, NX), BF16),
            jax.ShapeDtypeStruct((NX, NX), BF16),
        ),
        in_specs=[smem] + [hbm] * 5,
        out_specs=(vmem,) * 2,
        scratch_shapes=[
            pltpu.VMEM((LEAF * NX, NX), BF16),
            pltpu.VMEM((LEAF * NX, NU), BF16),
            pltpu.VMEM((1, LEAF), BF16),
            pltpu.VMEM((1, NX), F32),
            pltpu.VMEM((1, NU), F32),
            pltpu.VMEM((6, H, H), F32),
            pltpu.VMEM((H, H), F32),
            pltpu.VMEM((NU, NX), F32),
            pltpu.SemaphoreType.DMA((2 * LEAF + 3,)),
        ],
        compiler_params=pltpu.CompilerParams(vmem_limit_bytes=VMEM_LIMIT),
        cost_estimate=pl.CostEstimate(
            flops=LEAF * NX * 2 * (NX + NU) ** 2, bytes_accessed=LEAF * NX * (NX + NU) * 2, transcendentals=0
        ),
        name="lower_nodes",
    )(count, leaf_s, leaf_u, leafw, sc, cc)


def gather_kernel(
    parent_ref, midw_ref, value_ref, mid_s, mid_u,
    total_ref, weight_ref,
    own_buf, other_buf, sib_buf, in_buf, out_buf, tile, sib_tile, in_tile, out_tile,
    sib_send, sib_recv, send_sem, recv_sem,
):
    row = lax.axis_index("row")
    col = lax.axis_index("col")
    z = col // 2
    core = lax.rem(col, 2)
    sibling = col + 1 - 2 * core
    dist = lax.rem(z + 8 - 4 * core, 8)
    is_target = dist == 0
    down = jnp.logical_and(dist >= 1, dist <= 4)
    up_col = 2 * lax.rem(z + 1, 8) + core
    down_col = 2 * lax.rem(z + 7, 8) + core
    next_col = jnp.where(down, down_col, up_col)
    side = jnp.where(dist == 7, 1, 0)
    has_up = jnp.logical_and(dist != 4, dist != 5)

    barrier = pltpu.get_barrier_semaphore()
    for peer in (sibling, up_col, down_col):
        pl.semaphore_signal(barrier, inc=1, device_id=(row, peer), device_id_type=MESH)
    weight = midw_ref[0]
    parent = parent_ref[0]
    w_own = jnp.where(parent == core, weight, 0.0)
    w_other = jnp.where(parent == core, 0.0, weight)

    def put(i, block):
        own_buf[i * H : (i + 1) * H, :] = w_own * block
        other_buf[i * H : (i + 1) * H, :] = (w_other * block).astype(BF16)

    node_term(value_ref, mid_s.at[0], mid_u.at[0], put)
    tile[...] = jnp.where(iota2((8, 128), 0) == parent, weight, 0.0)
    pl.semaphore_wait(barrier, 3)

    def chunk(c):
        return pl.ds(pl.multiple_of(c * CHUNK, 16), CHUNK)

    def remote(src, dst, send, recv, peer):
        return pltpu.make_async_remote_copy(
            src_ref=src, dst_ref=dst, send_sem=send, recv_sem=recv,
            device_id=(row, peer), device_id_type=MESH,
        )

    def sib_copy(c):
        return remote(
            other_buf.at[chunk(c)], sib_buf.at[chunk(c)], sib_send.at[c], sib_recv.at[c], sibling
        )

    def chain_copy(c, to_side):
        return remote(
            out_buf.at[chunk(c)], in_buf.at[to_side, chunk(c)],
            send_sem.at[c], recv_sem.at[to_side, c], next_col,
        )

    def sib_tile_copy():
        return remote(tile, sib_tile, sib_send.at[N_CHUNK], sib_recv.at[N_CHUNK], sibling)

    def tile_copy(to_side):
        return remote(
            out_tile, in_tile.at[to_side],
            send_sem.at[N_CHUNK], recv_sem.at[to_side, N_CHUNK], next_col,
        )

    def start_sib(c, carry):
        sib_copy(c).start()
        return carry

    lax.fori_loop(0, N_CHUNK, start_sib, 0)
    sib_tile_copy().start()

    def step(c, carry):
        rows = chunk(c)
        sib_copy(c).wait_recv()
        part = own_buf[rows, :] + sib_buf[rows, :].astype(F32)

        @pl.when(jnp.logical_not(has_up))
        def _():
            out_buf[rows, :] = part.astype(BF16)
            chain_copy(c, side).start()

        @pl.when(has_up)
        def _():
            chain_copy(c, 0).wait_recv()
            more = part + in_buf[0, rows, :].astype(F32)

            @pl.when(is_target)
            def _():
                chain_copy(c, 1).wait_recv()
                total_ref[rows, :] = more + in_buf[1, rows, :].astype(F32)

            @pl.when(jnp.logical_not(is_target))
            def _():
                out_buf[rows, :] = more.astype(BF16)
                chain_copy(c, side).start()

        return carry

    lax.fori_loop(0, N_CHUNK, step, 0)
    sib_tile_copy().wait_recv()
    tiles = tile[...] + sib_tile[...]

    @pl.when(jnp.logical_not(has_up))
    def _():
        out_tile[...] = tiles
        tile_copy(side).start()

    @pl.when(has_up)
    def _():
        tile_copy(0).wait_recv()
        more = tiles + in_tile[0]

        @pl.when(is_target)
        def _():
            tile_copy(1).wait_recv()
            weight_ref[...] = more + in_tile[1]

        @pl.when(jnp.logical_not(is_target))
        def _():
            out_tile[...] = more
            tile_copy(side).start()

    def drain(c, carry):
        sib_copy(c).wait_send()

        @pl.when(jnp.logical_not(is_target))
        def _():
            chain_copy(c, side).wait_send()

        return carry

    lax.fori_loop(0, N_CHUNK, drain, 0)
    sib_tile_copy().wait_send()

    @pl.when(jnp.logical_not(is_target))
    def _():
        tile_copy(side).wait_send()


def gather(parent, midw, value, mid_s, mid_u):
    smem = pl.BlockSpec(memory_space=pltpu.SMEM)
    vmem = pl.BlockSpec(memory_space=pltpu.VMEM)
    dma = pltpu.SemaphoreType.DMA
    return pl.pallas_call(
        gather_kernel,
        out_shape=(
            jax.ShapeDtypeStruct((ROWS, H), F32),
            jax.ShapeDtypeStruct((8, 128), F32),
        ),
        in_specs=[smem, smem, vmem, vmem, vmem],
        out_specs=(vmem,) * 2,
        scratch_shapes=[
            pltpu.VMEM((ROWS, H), F32),
            pltpu.VMEM((ROWS, H), BF16),
            pltpu.VMEM((ROWS, H), BF16),
            pltpu.VMEM((2, ROWS, H), BF16),
            pltpu.VMEM((ROWS, H), BF16),
            pltpu.VMEM((8, 128), F32),
            pltpu.VMEM((8, 128), F32),
            pltpu.VMEM((2, 8, 128), F32),
            pltpu.VMEM((8, 128), F32),
            dma((N_CHUNK + 1,)),
            dma((N_CHUNK + 1,)),
            dma((N_CHUNK + 1,)),
            dma((2, N_CHUNK + 1)),
        ],
        compiler_params=pltpu.CompilerParams(
            collective_id=0, has_side_effects=True, vmem_limit_bytes=VMEM_LIMIT
        ),
        name="group_sum",
    )(parent, midw, value, mid_s, mid_u)


def upper_kernel(total_ref, weight_ref, sc_ref, cc_ref, gv_ref, blocks, work, feed):
    col = lax.axis_index("col")
    core = lax.rem(col, 2)

    @pl.when(col == 9 * core)
    def _():
        picked = jnp.where(iota2((8, 128), 0) == core, weight_ref[...], 0.0)
        scale = 1.0 / jnp.sum(picked, axis=0, keepdims=True)[:, :1]
        for i in range(6):
            blocks[i] = total_ref[i * H : (i + 1) * H, :] * scale
        gain_ref = gv_ref.at[pl.ds(0, NU)]
        value_ref = gv_ref.at[pl.ds(NU, NX)]
        riccati(lambda i: blocks[i], sc_ref[...], cc_ref[...], gain_ref, value_ref, work, feed)


def upper(total, weight, sc, cc):
    vmem = pl.BlockSpec(memory_space=pltpu.VMEM)
    return pl.pallas_call(
        upper_kernel,
        out_shape=jax.ShapeDtypeStruct((GV_ROWS, NX), BF16),
        in_specs=[vmem] * 4,
        out_specs=vmem,
        scratch_shapes=[
            pltpu.VMEM((6, H, H), F32),
            pltpu.VMEM((H, H), F32),
            pltpu.VMEM((NU, NX), F32),
        ],
        compiler_params=pltpu.CompilerParams(vmem_limit_bytes=VMEM_LIMIT),
        name="upper_nodes",
    )(total, weight, sc, cc)


def root_kernel(
    upw_ref, gv_ref, up_s, up_u, gvs_ref, total_ref, wtiles_ref,
    term_ref, wtile_ref, in_buf, piece_buf, pair_buf,
    w_send, w_recv, a_send, a_recv, b_send, b_recv, c_send, c_recv, s_send, s_recv,
    g_send, g_recv, gs_send, gs_recv,
):
    row = lax.axis_index("row")
    col = lax.axis_index("col")
    z = col // 2
    core = lax.rem(col, 2)
    sibling = col + 1 - 2 * core
    dist = lax.rem(z + 8 - 4 * core, 8)
    is_target = dist == 0
    barrier = pltpu.get_barrier_semaphore()

    def greet(k, carry):
        pl.semaphore_signal(
            barrier, inc=1, device_id=(row, lax.rem(col + k, 16)), device_id_type=MESH
        )
        pl.semaphore_signal(
            barrier, inc=1, device_id=(lax.rem(row + k, 16), col), device_id_type=MESH
        )
        return carry

    lax.fori_loop(1, 16, greet, 0)
    wtile_ref[...] = jnp.full((8, 128), upw_ref[0] + upw_ref[1], F32)

    @pl.when(is_target)
    def _():
        gvs_ref[pl.ds(core, 1)] = gv_ref[...][None]
        up_weight = jnp.where(core == 0, upw_ref[0], upw_ref[1])

        def put(i, block):
            term_ref[i * H : (i + 1) * H, :] = (up_weight * block).astype(BF16)

        node_term(gv_ref.at[pl.ds(NU, NX)], up_s.at[core], up_u.at[core], put)

    pl.semaphore_wait(barrier, 30)

    def a_copy(to_row, at):
        return pltpu.make_async_remote_copy(
            src_ref=term_ref.at[pl.ds(pl.multiple_of(to_row * PIECE, 16), PIECE)],
            dst_ref=in_buf.at[at],
            send_sem=a_send.at[to_row],
            recv_sem=a_recv.at[at],
            device_id=(to_row, col),
            device_id_type=MESH,
        )

    def b_copy(to_col, slot):
        half = lax.rem(to_col, 2)
        return pltpu.make_async_remote_copy(
            src_ref=piece_buf.at[half],
            dst_ref=pair_buf.at[slot],
            send_sem=b_send.at[to_col],
            recv_sem=b_recv.at[slot],
            device_id=(row, to_col),
            device_id_type=MESH,
        )

    def c_copy(to_row, at):
        return pltpu.make_async_remote_copy(
            src_ref=total_ref.at[at, core],
            dst_ref=total_ref.at[at, core],
            send_sem=c_send.at[to_row],
            recv_sem=c_recv.at[at],
            device_id=(to_row, col),
            device_id_type=MESH,
        )

    def s_copy(at, half):
        return pltpu.make_async_remote_copy(
            src_ref=total_ref.at[at, half],
            dst_ref=total_ref.at[at, half],
            send_sem=s_send.at[at],
            recv_sem=s_recv.at[at],
            device_id=(row, sibling),
            device_id_type=MESH,
        )

    def w_copy(to_row, at):
        return pltpu.make_async_remote_copy(
            src_ref=wtile_ref,
            dst_ref=wtiles_ref.at[at],
            send_sem=w_send.at[to_row],
            recv_sem=w_recv.at[at],
            device_id=(to_row, col),
            device_id_type=MESH,
        )

    def g_rows(c):
        return pl.ds(pl.multiple_of(c * GV_CHUNK, 16), GV_CHUNK)

    def g_copy(c, slot, to_col, lane_id):
        return pltpu.make_async_remote_copy(
            src_ref=gvs_ref.at[slot, g_rows(c)],
            dst_ref=gvs_ref.at[slot, g_rows(c)],
            send_sem=g_send.at[lane_id, c],
            recv_sem=g_recv.at[c],
            device_id=(row, to_col),
            device_id_type=MESH,
        )

    def gs_copy(c, slot):
        return pltpu.make_async_remote_copy(
            src_ref=gvs_ref.at[slot, g_rows(c)],
            dst_ref=gvs_ref.at[slot, g_rows(c)],
            send_sem=gs_send.at[c],
            recv_sem=gs_recv.at[c],
            device_id=(row, sibling),
            device_id_type=MESH,
        )

    def peers(body):
        def one(k, carry):
            body(lax.rem(row + k, 16))
            return carry

        lax.fori_loop(1, 16, one, 0)

    def columns(body):
        def one(k, carry):
            body(lax.rem(col + k, 16))
            return carry

        lax.fori_loop(1, 16, one, 0)

    def gv_chunks(body, first=0, last=N_GV):
        def one(c, carry):
            body(c)
            return carry

        lax.fori_loop(first, last, one, 0)

    up_col = 2 * lax.rem(z + 1, 8) + core
    down_col = 2 * lax.rem(z + 7, 8) + core
    to_up = dist <= 3
    to_down = jnp.logical_or(dist == 0, dist >= 6)

    def forward(c):
        @pl.when(to_up)
        def _():
            g_copy(c, core, up_col, 0).start()

        @pl.when(to_down)
        def _():
            g_copy(c, core, down_col, 1).start()

        gs_copy(c, core).start()

    @pl.when(is_target)
    def _():
        peers(lambda p: a_copy(p, row).start())

    peers(lambda p: w_copy(p, row).start())

    @pl.when(is_target)
    def _():
        gv_chunks(forward)
        acc = term_ref[pl.ds(pl.multiple_of(row * PIECE, 16), PIECE), :].astype(F32)

        def add(k, acc):
            source = lax.rem(row + k, 16)
            a_copy(source, source).wait_recv()
            return acc + in_buf[source].astype(F32)

        acc = lax.fori_loop(1, 16, add, acc)
        piece = acc.astype(BF16)
        piece_buf[0] = piece[:HALF]
        piece_buf[1] = piece[HALF:]
        columns(lambda p: b_copy(p, core).start())
        pair_buf[pl.ds(core, 1)] = piece_buf[pl.ds(core, 1)]
        b_copy(col, 1 - core).wait_recv()

    def relay(c):
        g_copy(c, core, up_col, 0).wait_recv()
        forward(c)

    hops = jnp.minimum(dist, 8 - dist)
    early = jnp.where(hops <= 2, N_GV, jnp.where(hops == 3, N_GV // 2, 0))

    @pl.when(jnp.logical_not(is_target))
    def _():
        gv_chunks(relay, 0, early)
        b_copy(col, 0).wait_recv()
        b_copy(col, 1).wait_recv()

    pair = pair_buf[0].astype(F32) + pair_buf[1].astype(F32)
    total_ref[pl.ds(row, 1), pl.ds(core, 1)] = pair.astype(BF16)[None, None]
    peers(lambda p: c_copy(p, row).start())
    s_copy(row, core).start()

    @pl.when(jnp.logical_not(is_target))
    def _():
        gv_chunks(relay, early, N_GV)

    def relay_piece(p):
        c_copy(p, p).wait_recv()
        s_copy(p, core).start()

    peers(relay_piece)

    def finish(at, carry):
        s_copy(at, 1 - core).wait_recv()
        s_copy(at, core).wait_send()
        return carry

    lax.fori_loop(0, 16, finish, 0)

    def finish_peer(p):
        c_copy(p, row).wait_send()
        w_copy(p, row).wait_send()
        w_copy(p, p).wait_recv()

    peers(finish_peer)
    wtiles_ref[pl.ds(row, 1)] = wtile_ref[...][None]

    @pl.when(is_target)
    def _():
        peers(lambda p: a_copy(p, row).wait_send())
        columns(lambda p: b_copy(p, core).wait_send())

    def finish_gv(c):
        gs_copy(c, 1 - core).wait_recv()
        gs_copy(c, core).wait_send()

        @pl.when(to_up)
        def _():
            g_copy(c, core, up_col, 0).wait_send()

        @pl.when(to_down)
        def _():
            g_copy(c, core, down_col, 1).wait_send()

    gv_chunks(finish_gv)


def root_sum(upw, gv, up_s, up_u):
    smem = pl.BlockSpec(memory_space=pltpu.SMEM)
    vmem = pl.BlockSpec(memory_space=pltpu.VMEM)
    dma = pltpu.SemaphoreType.DMA
    return pl.pallas_call(
        root_kernel,
        out_shape=(
            jax.ShapeDtypeStruct((2, GV_ROWS, NX), BF16),
            jax.ShapeDtypeStruct((16, 2, HALF, H), BF16),
            jax.ShapeDtypeStruct((16, 8, 128), F32),
        ),
        in_specs=[smem, vmem, vmem, vmem],
        out_specs=(vmem,) * 3,
        scratch_shapes=[
            pltpu.VMEM((ROWS, H), BF16),
            pltpu.VMEM((8, 128), F32),
            pltpu.VMEM((16, PIECE, H), BF16),
            pltpu.VMEM((2, HALF, H), BF16),
            pltpu.VMEM((2, HALF, H), BF16),
            dma((16,)), dma((16,)),
            dma((16,)), dma((16,)),
            dma((16,)), dma((2,)),
            dma((16,)), dma((16,)),
            dma((16,)), dma((16,)),
            dma((2, N_GV)), dma((N_GV,)),
            dma((N_GV,)), dma((N_GV,)),
        ],
        compiler_params=pltpu.CompilerParams(
            collective_id=1, has_side_effects=True, vmem_limit_bytes=VMEM_LIMIT
        ),
        name="root_sum",
    )(upw, gv, up_s, up_u)


def down_kernel(
    count_ref, parent_ref, gvs_ref, total_ref, wtiles_ref, mid_gain_ref, mid_value_ref, root_cov_ref,
    up_s, up_u, mid_s, mid_u, leaf_s, leaf_u, sc_ref, cc_ref, nc_ref,
    root_gain_out, root_value_out, up_gain_out, up_value_out, up_cov_out,
    mid_gain_out, mid_value_out, mid_cov_out, leaf_cov_out,
    root_gain_ref, root_value_ref, up_cov_ref, mid_cov_ref, lcov, blocks, work, feed, out_sems,
):
    outs = []

    def emit(src, dst):
        copy = pltpu.make_async_copy(src, dst, out_sems.at[len(outs)])
        copy.start()
        outs.append(copy)

    for s in range(2):
        emit(gvs_ref.at[s, pl.ds(0, NU)], up_gain_out.at[s])
        emit(gvs_ref.at[s, pl.ds(NU, NX)], up_value_out.at[s])
    emit(mid_gain_ref, mid_gain_out)
    emit(mid_value_ref, mid_value_out)
    weight = jnp.sum(wtiles_ref[...], axis=0)
    scale = 1.0 / weight[:1, :1]
    for i in range(6):
        blocks[i] = total_ref[i * H : (i + 1) * H, :].astype(F32) * scale
    riccati(
        lambda i: blocks[i], sc_ref[...], cc_ref[...], root_gain_ref, root_value_ref, work, feed
    )
    emit(root_gain_ref, root_gain_out)
    emit(root_value_ref, root_value_out)
    noise = nc_ref[...]
    root_gain = root_gain_ref[...]
    root_cov = root_cov_ref[...]
    for s in range(2):
        store_cov(up_cov_ref.at[s], propagate(root_cov, root_gain, up_s[s], up_u[s], noise))
        emit(up_cov_ref.at[s], up_cov_out.at[s])
    parent = parent_ref[0]
    store_cov(
        mid_cov_ref,
        propagate(up_cov_ref[parent], gvs_ref[parent, :NU, :], mid_s[0], mid_u[0], noise),
    )
    emit(mid_cov_ref, mid_cov_out)
    live = count_ref[0]
    mid_cov = mid_cov_ref[...]
    mid_gain = mid_gain_ref[...]
    for c in range(LEAF):
        keep = c < live
        result = propagate(mid_cov, mid_gain, leaf_s[c], leaf_u[c], noise)
        store_cov(lcov.at[c], [jnp.where(keep, block, jnp.zeros_like(block)) for block in result])
        emit(lcov.at[c], leaf_cov_out.at[c])
    for out in outs:
        out.wait()


def down(count, parent, *arrays):
    smem = pl.BlockSpec(memory_space=pltpu.SMEM)
    vmem = pl.BlockSpec(memory_space=pltpu.VMEM)
    hbm = pl.BlockSpec(memory_space=pl.ANY)
    return pl.pallas_call(
        down_kernel,
        out_shape=(
            jax.ShapeDtypeStruct((NU, NX), BF16),
            jax.ShapeDtypeStruct((NX, NX), BF16),
            jax.ShapeDtypeStruct((2, NU, NX), BF16),
            jax.ShapeDtypeStruct((2, NX, NX), BF16),
            jax.ShapeDtypeStruct((2, NX, NX), BF16),
            jax.ShapeDtypeStruct((NU, NX), BF16),
            jax.ShapeDtypeStruct((NX, NX), BF16),
            jax.ShapeDtypeStruct((NX, NX), BF16),
            jax.ShapeDtypeStruct((LEAF, NX, NX), BF16),
        ),
        in_specs=[smem, smem] + [vmem] * len(arrays),
        out_specs=(hbm,) * 9,
        scratch_shapes=[
            pltpu.VMEM((NU, NX), BF16),
            pltpu.VMEM((NX, NX), BF16),
            pltpu.VMEM((2, NX, NX), BF16),
            pltpu.VMEM((NX, NX), BF16),
            pltpu.VMEM((LEAF, NX, NX), BF16),
            pltpu.VMEM((6, H, H), F32),
            pltpu.VMEM((H, H), F32),
            pltpu.VMEM((NU, NX), F32),
            pltpu.SemaphoreType.DMA((15,)),
        ],
        compiler_params=pltpu.CompilerParams(vmem_limit_bytes=VMEM_LIMIT),
        name="down_sweep",
    )(count, parent, *arrays)


def local(
    leaf_state_map,
    leaf_input_map,
    leaf_weight,
    leaf_count,
    mid_state_map,
    mid_input_map,
    mid_weight,
    mid_parent,
    up_state_map,
    up_input_map,
    up_weight,
    root_cov,
    state_cost,
    control_cost,
    noise_cov,
):
    sc = state_cost.reshape(1, NX)
    cc = control_cost.reshape(1, NU)
    nc = noise_cov.reshape(1, NX)
    mid_gain, mid_value = lower(
        leaf_count, leaf_state_map, leaf_input_map, leaf_weight.reshape(1, LEAF), sc, cc
    )
    total, weight = gather(mid_parent, mid_weight, mid_value, mid_state_map, mid_input_map)
    gv = upper(total, weight, sc, cc)
    gvs, root_total, wtiles = root_sum(up_weight, gv, up_state_map, up_input_map)
    outs = down(
        leaf_count, mid_parent, gvs, root_total.reshape(ROWS, H), wtiles, mid_gain, mid_value,
        root_cov, up_state_map, up_input_map, mid_state_map, mid_input_map,
        leaf_state_map, leaf_input_map, sc, cc, nc,
    )
    root_gain, root_value, up_gain, up_value, up_cov, mid_gain, mid_value, mid_cov, leaf_cov = outs
    return (
        root_gain,
        root_value,
        up_gain,
        up_value,
        up_cov,
        mid_gain[None],
        mid_value[None],
        mid_cov[None],
        leaf_cov,
    )


def solution(mesh):
    both = P(("row", "col"))
    return jax.shard_map(
        local,
        mesh=mesh,
        in_specs=(
            both, both, both, both, both, both, both, both,
            P("row"), P("row"), P("row"), P(), P(), P(), P(),
        ),
        out_specs=(P(), P(), P("row"), P("row"), P("row"), both, both, both, both),
        check_vma=False,
    )
```

```python
import functools

import jax
import jax.numpy as jnp
from jax import lax
from jax.experimental import pallas as pl
from jax.experimental.pallas import tpu as pltpu
from jax.sharding import PartitionSpec as P

NX = 512
NU = 256
H = 256
LEAF = 4
ROWS = 6 * H
BLOCKS = ((0, 0), (1, 0), (1, 1), (2, 0), (2, 1), (2, 2))
F32 = jnp.float32
BF16 = jnp.bfloat16
MESH = pl.DeviceIdType.MESH
VMEM_LIMIT = 24 * 1024 * 1024
N_CHUNK = 24
CHUNK = ROWS // N_CHUNK
N_GV = 12
GV_ROWS = NX + NU
GV_CHUNK = GV_ROWS // N_GV
PIECE = ROWS // 16
HALF = PIECE // 2
ERROR_TOL = 1e-4
MAX_CONTRACTION = 0.25
MAX_RATIO = 256.0
MAX_REFINE = 8


def mm(a, b):
    return jnp.dot(a, b, preferred_element_type=F32)


def mm_tn(a, b):
    return lax.dot_general(a, b, (((0,), (0,)), ((), ())), preferred_element_type=F32)


def mm_nt(a, b):
    return lax.dot_general(a, b, (((1,), (1,)), ((), ())), preferred_element_type=F32)


def split(a):
    hi = a.astype(BF16)
    return hi, (a - hi.astype(F32)).astype(BF16)


def iota2(shape, dim):
    return lax.broadcasted_iota(jnp.int32, shape, dim)


def eye_mask(n):
    return iota2((n, n), 0) == iota2((n, n), 1)


def to_column(row):
    n = row.shape[1]
    parts = []
    for i in range(n // 128):
        block = jnp.broadcast_to(row[:, i * 128 : (i + 1) * 128], (128, 128))
        parts.append(jnp.sum(jnp.where(eye_mask(128), block, 0.0), axis=1, keepdims=True))
    return jnp.concatenate(parts, axis=0)


def add_diag(block, row):
    return block + jnp.where(eye_mask(block.shape[0]), row, 0.0)


def all_sum(a):
    return jnp.sum(jnp.sum(a, axis=1, keepdims=True), axis=0, keepdims=True)


def riccati(get, state_row, control_row, gain_ref, value_ref, work, feed):
    hess = add_diag(get(5), control_row)
    ba = jnp.concatenate([get(3), get(4)], axis=1)
    eye = eye_mask(H)
    upper = jnp.max(jnp.max(jnp.sum(jnp.abs(hess), axis=1, keepdims=True), axis=0, keepdims=True))
    lower = jnp.minimum(jnp.min(control_row), upper)
    mid = 0.5 * (upper + lower)
    rad = 0.5 * (upper - lower)
    den = 2.0 * mid * mid - rad * rad
    error0 = rad * rad / den
    steps = jnp.int32(0)
    for j in range(16):
        steps += (error0 > 0.1 ** (0.5**j)).astype(jnp.int32)
    h_hi, h_lo = split(hess)
    ba_hi, ba_lo = split(ba)
    work[...] = jnp.where(eye, 4.0 * mid / den, 0.0) - (2.0 / den) * hess

    def newton(_, carry):
        x_hi = work[...].astype(BF16)
        res = jnp.where(eye, 1.0, 0.0) - mm(h_hi, x_hi)
        work[...] = x_hi.astype(F32) + mm(x_hi, res.astype(BF16))
        return carry

    lax.fori_loop(0, steps, newton, 0)
    x_hi = work[...].astype(BF16)
    res = (jnp.where(eye, 1.0, 0.0) - mm(h_hi, x_hi)) - mm(h_lo, x_hi)
    inv, inv_lo = split(x_hi.astype(F32) + mm(x_hi, res.astype(BF16)))
    feed[...] = -(mm(inv, ba_hi) + (mm(inv, ba_lo) + mm(inv_lo, ba_hi)))

    def unconverged(state):
        count, done, _ = state
        return jnp.logical_and(count < MAX_REFINE, done == 0)

    def refine(state):
        count, _, last = state
        f = feed[...]
        f_hi, f_lo = split(f)
        res = ba + (mm(h_hi, f_hi) + (mm(h_hi, f_lo) + mm(h_lo, f_hi)))
        step = mm(inv, res.astype(BF16))
        new = f - step
        feed[...] = new
        size = jnp.sum(step * step)
        norm = jnp.sum(new * new)
        last = jnp.where(count == 0, norm, last)
        small = jnp.logical_and(
            size <= MAX_CONTRACTION**2 * last, size * size <= ERROR_TOL**2 * norm * last
        )
        return count + 1, small.astype(jnp.int32), size

    first = (upper > MAX_RATIO * lower).astype(jnp.int32) * MAX_REFINE
    _, done, _ = lax.while_loop(unconverged, refine, (first, jnp.int32(0), jnp.float32(0.0)))

    @pl.when(done == 0)
    def _():
        work[...] = hess

        def sweep(k, carry):
            a = work[...]
            row = work[pl.ds(k, 1), :]
            here = iota2((H, H), 1) == k
            col = jnp.sum(jnp.where(here, a, 0.0), axis=1, keepdims=True)
            lane_k = iota2((1, H), 1) == k
            sub_k = iota2((H, 1), 0) == k
            pivot = jnp.sum(jnp.where(lane_k, row, 0.0), axis=1, keepdims=True)
            inv_p = 1.0 / pivot
            col0 = jnp.where(sub_k, 0.0, col)
            row1 = jnp.where(lane_k, 1.0, row) * inv_p
            base = jnp.where(jnp.logical_or(here, sub_k), 0.0, a)
            work[...] = jnp.where(sub_k, row1, base - col0 * row1)
            return carry

        lax.fori_loop(0, H, sweep, 0)
        feed[...] = -jnp.dot(
            work[...], ba, preferred_element_type=F32, precision=lax.Precision.HIGHEST
        )

    f = feed[...]
    f_hi, f_lo = split(f)
    gain_ref[...] = f_hi

    def quad(i, j):
        a = slice(i * H, (i + 1) * H)
        b = slice(j * H, (j + 1) * H)
        return mm_tn(ba_hi[:, a], f_hi[:, b]) + (
            mm_tn(ba_hi[:, a], f_lo[:, b]) + mm_tn(ba_lo[:, a], f_hi[:, b])
        )

    value_ref[:H, :H] = add_diag(get(0) + quad(0, 0), state_row[:, :H]).astype(BF16)
    cross = get(1) + quad(1, 0)
    value_ref[H:, :H] = cross.astype(BF16)
    value_ref[:H, H:] = cross.T.astype(BF16)
    value_ref[H:, H:] = add_diag(get(2) + quad(1, 1), state_row[:, H:]).astype(BF16)


def node_term(value_ref, state_ref, input_ref, put):
    value = value_ref[...]
    xs = [state_ref[:, :H], state_ref[:, H:], input_ref[...]]
    ys = [mm(value, x).astype(BF16) for x in xs]
    for i, (a, b) in enumerate(BLOCKS):
        put(i, mm_tn(xs[a], ys[b]))


def propagate(cov, gain, state, inputs, noise_row):
    closed = (state.astype(F32) + mm(inputs, gain)).astype(BF16)
    moved = mm(closed, cov).astype(BF16)
    top = mm_nt(moved[:H], closed[:H])
    cross = mm_nt(moved[H:], closed[:H])
    low = mm_nt(moved[H:], closed[H:])
    return (
        add_diag(top, noise_row[:, :H]).astype(BF16),
        cross.astype(BF16),
        cross.T.astype(BF16),
        add_diag(low, noise_row[:, H:]).astype(BF16),
    )


def store_cov(ref, blocks):
    ref[:H, :H] = blocks[0]
    ref[H:, :H] = blocks[1]
    ref[:H, H:] = blocks[2]
    ref[H:, H:] = blocks[3]


def lane(row, k):
    return jnp.sum(jnp.where(iota2(row.shape, 1) == k, row, 0.0), axis=1, keepdims=True)


def lower_kernel(
    count_ref, leaf_s, leaf_u, leafw_in, sc_in, cc_in,
    gain_ref, value_ref,
    ls, lu, leafw_ref, sc_ref, cc_ref, total, work, feed, sems,
):
    copies = []
    small = []
    for i, (src, dst) in enumerate(((leafw_in, leafw_ref), (sc_in, sc_ref), (cc_in, cc_ref))):
        small.append(pltpu.make_async_copy(src, dst, sems.at[2 * LEAF + i]))
        small[-1].start()
    for c in range(LEAF):
        copies.append(pltpu.make_async_copy(leaf_s.at[c], ls.at[pl.ds(c * NX, NX)], sems.at[2 * c]))
        copies.append(pltpu.make_async_copy(leaf_u.at[c], lu.at[pl.ds(c * NX, NX)], sems.at[2 * c + 1]))
    for copy in copies:
        copy.start()
    for copy in small:
        copy.wait()
    live = count_ref[0]
    weights = leafw_ref[...].astype(F32)
    weights = jnp.where(iota2(weights.shape, 1) < live, weights, 0.0)
    weights = weights / jnp.sum(weights, axis=1, keepdims=True)
    cost = to_column(sc_ref[...])
    for c in range(LEAF):
        copies[2 * c].wait()
        copies[2 * c + 1].wait()
        scale = cost * lane(weights, c)
        rows = slice(c * NX, (c + 1) * NX)
        xs = [ls[rows, :H], ls[rows, H:], lu[rows, :]]
        ss = [(scale * x.astype(F32)).astype(BF16) for x in xs]
        for i, (a, b) in enumerate(BLOCKS):
            part = mm_tn(xs[a], ss[b])
            if c == 0:
                total[i] = part
            else:
                total[i] += part
    riccati(lambda i: total[i], sc_ref[...], cc_ref[...], gain_ref, value_ref, work, feed)


def lower(count, leaf_s, leaf_u, leafw, sc, cc):
    smem = pl.BlockSpec(memory_space=pltpu.SMEM)
    vmem = pl.BlockSpec(memory_space=pltpu.VMEM)
    hbm = pl.BlockSpec(memory_space=pltpu.HBM)
    leaf_s, leaf_u, leafw, sc, cc = [
        pltpu.with_memory_space_constraint(a, pltpu.HBM) for a in (leaf_s, leaf_u, leafw, sc, cc)
    ]
    return pl.pallas_call(
        lower_kernel,
        out_shape=(
            jax.ShapeDtypeStruct((NU, NX), BF16),
            jax.ShapeDtypeStruct((NX, NX), BF16),
        ),
        in_specs=[smem] + [hbm] * 5,
        out_specs=(vmem,) * 2,
        scratch_shapes=[
            pltpu.VMEM((LEAF * NX, NX), BF16),
            pltpu.VMEM((LEAF * NX, NU), BF16),
            pltpu.VMEM((1, LEAF), BF16),
            pltpu.VMEM((1, NX), F32),
            pltpu.VMEM((1, NU), F32),
            pltpu.VMEM((6, H, H), F32),
            pltpu.VMEM((H, H), F32),
            pltpu.VMEM((NU, NX), F32),
            pltpu.SemaphoreType.DMA((2 * LEAF + 3,)),
        ],
        compiler_params=pltpu.CompilerParams(vmem_limit_bytes=VMEM_LIMIT),
        cost_estimate=pl.CostEstimate(
            flops=LEAF * NX * 2 * (NX + NU) ** 2, bytes_accessed=LEAF * NX * (NX + NU) * 2, transcendentals=0
        ),
        name="lower_nodes",
    )(count, leaf_s, leaf_u, leafw, sc, cc)


def gather_kernel(
    parent_ref, midw_ref, value_ref, mid_s, mid_u,
    total_ref, weight_ref,
    own_buf, other_buf, sib_buf, in_buf, out_buf, tile, sib_tile, in_tile, out_tile,
    sib_send, sib_recv, send_sem, recv_sem,
):
    row = lax.axis_index("row")
    col = lax.axis_index("col")
    z = col // 2
    core = lax.rem(col, 2)
    sibling = col + 1 - 2 * core
    dist = lax.rem(z + 8 - 4 * core, 8)
    is_target = dist == 0
    down = jnp.logical_and(dist >= 1, dist <= 4)
    up_col = 2 * lax.rem(z + 1, 8) + core
    down_col = 2 * lax.rem(z + 7, 8) + core
    next_col = jnp.where(down, down_col, up_col)
    side = jnp.where(dist == 7, 1, 0)
    has_up = jnp.logical_and(dist != 4, dist != 5)

    barrier = pltpu.get_barrier_semaphore()
    for peer in (sibling, up_col, down_col):
        pl.semaphore_signal(barrier, inc=1, device_id=(row, peer), device_id_type=MESH)
    weight = midw_ref[0]
    parent = parent_ref[0]
    w_own = jnp.where(parent == core, weight, 0.0)
    w_other = jnp.where(parent == core, 0.0, weight)

    def put(i, block):
        own_buf[i * H : (i + 1) * H, :] = w_own * block
        other_buf[i * H : (i + 1) * H, :] = (w_other * block).astype(BF16)

    node_term(value_ref, mid_s.at[0], mid_u.at[0], put)
    tile[...] = jnp.where(iota2((8, 128), 0) == parent, weight, 0.0)
    pl.semaphore_wait(barrier, 3)

    def chunk(c):
        return pl.ds(pl.multiple_of(c * CHUNK, 16), CHUNK)

    def remote(src, dst, send, recv, peer):
        return pltpu.make_async_remote_copy(
            src_ref=src, dst_ref=dst, send_sem=send, recv_sem=recv,
            device_id=(row, peer), device_id_type=MESH,
        )

    def sib_copy(c):
        return remote(
            other_buf.at[chunk(c)], sib_buf.at[chunk(c)], sib_send.at[c], sib_recv.at[c], sibling
        )

    def chain_copy(c, to_side):
        return remote(
            out_buf.at[chunk(c)], in_buf.at[to_side, chunk(c)],
            send_sem.at[c], recv_sem.at[to_side, c], next_col,
        )

    def sib_tile_copy():
        return remote(tile, sib_tile, sib_send.at[N_CHUNK], sib_recv.at[N_CHUNK], sibling)

    def tile_copy(to_side):
        return remote(
            out_tile, in_tile.at[to_side],
            send_sem.at[N_CHUNK], recv_sem.at[to_side, N_CHUNK], next_col,
        )

    def start_sib(c, carry):
        sib_copy(c).start()
        return carry

    lax.fori_loop(0, N_CHUNK, start_sib, 0)
    sib_tile_copy().start()

    def step(c, carry):
        rows = chunk(c)
        sib_copy(c).wait_recv()
        part = own_buf[rows, :] + sib_buf[rows, :].astype(F32)

        @pl.when(jnp.logical_not(has_up))
        def _():
            out_buf[rows, :] = part.astype(BF16)
            chain_copy(c, side).start()

        @pl.when(has_up)
        def _():
            chain_copy(c, 0).wait_recv()
            more = part + in_buf[0, rows, :].astype(F32)

            @pl.when(is_target)
            def _():
                chain_copy(c, 1).wait_recv()
                total_ref[rows, :] = more + in_buf[1, rows, :].astype(F32)

            @pl.when(jnp.logical_not(is_target))
            def _():
                out_buf[rows, :] = more.astype(BF16)
                chain_copy(c, side).start()

        return carry

    lax.fori_loop(0, N_CHUNK, step, 0)
    sib_tile_copy().wait_recv()
    tiles = tile[...] + sib_tile[...]

    @pl.when(jnp.logical_not(has_up))
    def _():
        out_tile[...] = tiles
        tile_copy(side).start()

    @pl.when(has_up)
    def _():
        tile_copy(0).wait_recv()
        more = tiles + in_tile[0]

        @pl.when(is_target)
        def _():
            tile_copy(1).wait_recv()
            weight_ref[...] = more + in_tile[1]

        @pl.when(jnp.logical_not(is_target))
        def _():
            out_tile[...] = more
            tile_copy(side).start()

    def drain(c, carry):
        sib_copy(c).wait_send()

        @pl.when(jnp.logical_not(is_target))
        def _():
            chain_copy(c, side).wait_send()

        return carry

    lax.fori_loop(0, N_CHUNK, drain, 0)
    sib_tile_copy().wait_send()

    @pl.when(jnp.logical_not(is_target))
    def _():
        tile_copy(side).wait_send()


def gather(parent, midw, value, mid_s, mid_u):
    smem = pl.BlockSpec(memory_space=pltpu.SMEM)
    vmem = pl.BlockSpec(memory_space=pltpu.VMEM)
    dma = pltpu.SemaphoreType.DMA
    return pl.pallas_call(
        gather_kernel,
        out_shape=(
            jax.ShapeDtypeStruct((ROWS, H), F32),
            jax.ShapeDtypeStruct((8, 128), F32),
        ),
        in_specs=[smem, smem, vmem, vmem, vmem],
        out_specs=(vmem,) * 2,
        scratch_shapes=[
            pltpu.VMEM((ROWS, H), F32),
            pltpu.VMEM((ROWS, H), BF16),
            pltpu.VMEM((ROWS, H), BF16),
            pltpu.VMEM((2, ROWS, H), BF16),
            pltpu.VMEM((ROWS, H), BF16),
            pltpu.VMEM((8, 128), F32),
            pltpu.VMEM((8, 128), F32),
            pltpu.VMEM((2, 8, 128), F32),
            pltpu.VMEM((8, 128), F32),
            dma((N_CHUNK + 1,)),
            dma((N_CHUNK + 1,)),
            dma((N_CHUNK + 1,)),
            dma((2, N_CHUNK + 1)),
        ],
        compiler_params=pltpu.CompilerParams(
            collective_id=0, has_side_effects=True, vmem_limit_bytes=VMEM_LIMIT
        ),
        name="group_sum",
    )(parent, midw, value, mid_s, mid_u)


def upper_kernel(total_ref, weight_ref, sc_ref, cc_ref, gv_ref, blocks, work, feed):
    col = lax.axis_index("col")
    core = lax.rem(col, 2)

    @pl.when(col == 9 * core)
    def _():
        picked = jnp.where(iota2((8, 128), 0) == core, weight_ref[...], 0.0)
        scale = 1.0 / jnp.sum(picked, axis=0, keepdims=True)[:, :1]
        for i in range(6):
            blocks[i] = total_ref[i * H : (i + 1) * H, :] * scale
        gain_ref = gv_ref.at[pl.ds(0, NU)]
        value_ref = gv_ref.at[pl.ds(NU, NX)]
        riccati(lambda i: blocks[i], sc_ref[...], cc_ref[...], gain_ref, value_ref, work, feed)


def upper(total, weight, sc, cc):
    vmem = pl.BlockSpec(memory_space=pltpu.VMEM)
    return pl.pallas_call(
        upper_kernel,
        out_shape=jax.ShapeDtypeStruct((GV_ROWS, NX), BF16),
        in_specs=[vmem] * 4,
        out_specs=vmem,
        scratch_shapes=[
            pltpu.VMEM((6, H, H), F32),
            pltpu.VMEM((H, H), F32),
            pltpu.VMEM((NU, NX), F32),
        ],
        compiler_params=pltpu.CompilerParams(vmem_limit_bytes=VMEM_LIMIT),
        name="upper_nodes",
    )(total, weight, sc, cc)


def hops(step):
    return min(step, 4 - step)


NEAR = sorted(
    [(dy, dx) for dy in range(4) for dx in range(4) if dy or dx],
    key=lambda step: hops(step[0]) + hops(step[1]),
)


def root_kernel(
    upw_ref, gv_ref, up_s, up_u, gvs_ref, total_ref, wtiles_ref,
    term_ref, wtile_ref, in_buf, piece_buf, pair_buf,
    w_send, w_recv, ws_send, ws_recv, a_send, a_recv, b_send, b_recv, c_send, c_recv,
    s_send, s_recv, g_send, g_recv, gs_send, gs_recv,
):
    row = lax.axis_index("row")
    col = lax.axis_index("col")
    z = col // 2
    core = lax.rem(col, 2)
    sibling = col + 1 - 2 * core
    dist = lax.rem(z + 8 - 4 * core, 8)
    is_target = dist == 0
    is_adder = dist == 4
    is_plain = jnp.logical_not(jnp.logical_or(is_target, is_adder))
    up_col = 2 * lax.rem(z + 1, 8) + core
    down_col = 2 * lax.rem(z + 7, 8) + core
    other_adder = 2 * lax.rem(z + 4, 8) + 1 - core
    slot = 1 - core
    barrier = pltpu.get_barrier_semaphore()

    def signal(to_row, to_col):
        pl.semaphore_signal(barrier, inc=1, device_id=(to_row, to_col), device_id_type=MESH)

    def peers(body):
        def one(k, carry):
            body(lax.rem(row + k, 16))
            return carry

        lax.fori_loop(1, 16, one, 0)

    def at_step(step):
        return lax.rem(row // 4 + step[0], 4) * 4 + lax.rem(lax.rem(row, 4) + step[1], 4)

    def far_first(body):
        for step in reversed(NEAR):
            body(at_step(step))

    def near_first(body):
        for step in NEAR:
            body(at_step(step))

    for to_col in (sibling, up_col, down_col):
        signal(row, to_col)

    @pl.when(is_target)
    def _():
        peers(lambda p: signal(p, sibling))

    @pl.when(is_adder)
    def _():
        peers(lambda p: signal(p, sibling))
        peers(lambda p: signal(p, col))
        signal(row, other_adder)
        for off in (1, 2, 3, 5, 6, 7):
            for half in range(2):
                signal(row, 2 * lax.rem(z + off, 8) + half)

    @pl.when(is_plain)
    def _():
        peers(lambda p: signal(p, col))
        signal(row, 1)
        signal(row, 8)

    wtile_ref[...] = jnp.full((8, 128), upw_ref[0] + upw_ref[1], F32)

    @pl.when(is_target)
    def _():
        gvs_ref[pl.ds(core, 1)] = gv_ref[...][None]
        up_weight = jnp.where(core == 0, upw_ref[0], upw_ref[1])

        def put(i, block):
            term_ref[i * H : (i + 1) * H, :] = (up_weight * block).astype(BF16)

        node_term(gv_ref.at[pl.ds(NU, NX)], up_s.at[core], up_u.at[core], put)
        pl.semaphore_wait(barrier, 18)

    @pl.when(is_adder)
    def _():
        pl.semaphore_wait(barrier, 46)

    @pl.when(is_plain)
    def _():
        pl.semaphore_wait(barrier, 20)

    def remote(src, dst, send, recv, to_row, to_col):
        return pltpu.make_async_remote_copy(
            src_ref=src, dst_ref=dst, send_sem=send, recv_sem=recv,
            device_id=(to_row, to_col), device_id_type=MESH,
        )

    def a_copy(to_row, at):
        return remote(
            term_ref.at[pl.ds(pl.multiple_of(to_row * PIECE, 16), PIECE)], in_buf.at[at],
            a_send.at[to_row], a_recv.at[at], to_row, sibling,
        )

    def b_half(off, half, of_slot):
        return remote(
            piece_buf.at[half], pair_buf.at[of_slot, half],
            b_send.at[2 * off + half], b_recv.at[of_slot], row, 2 * lax.rem(z + off, 8) + half,
        )

    def b_whole(of_slot):
        return remote(
            piece_buf, pair_buf.at[of_slot], b_send.at[0], b_recv.at[of_slot], row, other_adder
        )

    def c_half(to_row, at):
        part = total_ref.at[at, core]
        return remote(part, part, c_send.at[to_row], c_recv.at[at], to_row, col)

    def c_whole(to_row, at):
        part = total_ref.at[at]
        return remote(part, part, c_send.at[to_row], c_recv.at[at], to_row, col)

    def s_half(at, half):
        part = total_ref.at[at, half]
        return remote(part, part, s_send.at[at], s_recv.at[at], row, sibling)

    def s_whole(at):
        part = total_ref.at[at]
        return remote(part, part, s_send.at[at], s_recv.at[at], row, sibling)

    def w_copy(to_row, at):
        return remote(wtile_ref, wtiles_ref.at[at], w_send.at[to_row], w_recv.at[at], to_row, col)

    def ws_copy():
        return remote(wtiles_ref, wtiles_ref, ws_send.at[0], ws_recv.at[0], row, sibling)

    def g_part(c, of_slot):
        return gvs_ref.at[of_slot, pl.ds(pl.multiple_of(c * GV_CHUNK, 16), GV_CHUNK)]

    def g_copy(c, to_col, way):
        part = g_part(c, core)
        return remote(part, part, g_send.at[way, c], g_recv.at[c], row, to_col)

    def gs_copy(c, of_slot):
        part = g_part(c, of_slot)
        return remote(part, part, gs_send.at[c], gs_recv.at[c], row, sibling)

    def gv_chunks(body, first=0, last=N_GV):
        def one(c, carry):
            body(c)
            return carry

        lax.fori_loop(first, last, one, 0)

    to_up = dist <= 3
    to_down = jnp.logical_or(dist == 0, dist >= 6)

    def forward(c):
        @pl.when(to_up)
        def _():
            g_copy(c, up_col, 0).start()

        @pl.when(to_down)
        def _():
            g_copy(c, down_col, 1).start()

        gs_copy(c, core).start()

    def relay(c):
        g_copy(c, up_col, 0).wait_recv()
        forward(c)

    def pieces(body):
        def one(at, carry):
            body(at)
            return carry

        lax.fori_loop(0, 16, one, 0)

    def send_tiles():
        peers(lambda p: w_copy(p, row).start())
        wtiles_ref[pl.ds(row, 1)] = wtile_ref[...][None]

    @pl.when(is_target)
    def _():
        far_first(lambda p: a_copy(p, row).start())
        a_copy(row, row).start()
        gv_chunks(forward)
        pieces(lambda at: s_whole(at).wait_recv())
        ws_copy().wait_recv()
        pieces(lambda p: a_copy(p, row).wait_send())

    @pl.when(is_adder)
    def _():
        send_tiles()
        a_copy(row, row).wait_recv()
        acc = in_buf[row].astype(F32)
        for step in NEAR:
            source = at_step(step)
            a_copy(source, source).wait_recv()
            acc = acc + in_buf[source].astype(F32)
        piece = acc.astype(BF16)
        piece_buf[0] = piece[:HALF]
        piece_buf[1] = piece[HALF:]
        b_whole(slot).start()
        for off in (3, 5, 2, 6, 1, 7):
            for half in range(2):
                b_half(off, half, slot).start()
        own = piece_buf[...].astype(F32)
        b_whole(core).wait_recv()
        pair = own + pair_buf[core].astype(F32)
        total_ref[pl.ds(row, 1)] = pair.astype(BF16)[None]
        far_first(lambda p: c_whole(p, row).start())
        s_whole(row).start()
        gv_chunks(relay)

        def relay_piece(p):
            c_whole(p, p).wait_recv()
            s_whole(p).start()

        near_first(relay_piece)
        peers(lambda p: w_copy(p, p).wait_recv())
        ws_copy().start()
        ws_copy().wait_send()
        pieces(lambda at: s_whole(at).wait_send())
        peers(lambda p: c_whole(p, row).wait_send())
        peers(lambda p: w_copy(p, row).wait_send())
        b_whole(slot).wait_send()
        for off in (3, 5, 2, 6, 1, 7):
            for half in range(2):
                b_half(off, half, slot).wait_send()

    steps = jnp.minimum(dist, 8 - dist)
    early = jnp.where(steps <= 2, N_GV, N_GV // 2)

    @pl.when(is_plain)
    def _():
        send_tiles()
        gv_chunks(relay, 0, early)
        b_half(1, core, 0).wait_recv()
        b_half(1, core, 1).wait_recv()
        pair = pair_buf[0, core].astype(F32) + pair_buf[1, core].astype(F32)
        total_ref[pl.ds(row, 1), pl.ds(core, 1)] = pair.astype(BF16)[None, None]
        far_first(lambda p: c_half(p, row).start())
        s_half(row, core).start()
        gv_chunks(relay, early, N_GV)

        def relay_piece(p):
            c_half(p, p).wait_recv()
            s_half(p, core).start()

        near_first(relay_piece)

        def finish(at):
            s_half(at, 1 - core).wait_recv()
            s_half(at, core).wait_send()

        pieces(finish)
        peers(lambda p: w_copy(p, p).wait_recv())
        peers(lambda p: c_half(p, row).wait_send())
        peers(lambda p: w_copy(p, row).wait_send())

    def finish_gv(c):
        gs_copy(c, 1 - core).wait_recv()
        gs_copy(c, core).wait_send()

        @pl.when(to_up)
        def _():
            g_copy(c, up_col, 0).wait_send()

        @pl.when(to_down)
        def _():
            g_copy(c, down_col, 1).wait_send()

    gv_chunks(finish_gv)


def root_sum(upw, gv, up_s, up_u):
    smem = pl.BlockSpec(memory_space=pltpu.SMEM)
    vmem = pl.BlockSpec(memory_space=pltpu.VMEM)
    dma = pltpu.SemaphoreType.DMA
    return pl.pallas_call(
        root_kernel,
        out_shape=(
            jax.ShapeDtypeStruct((2, GV_ROWS, NX), BF16),
            jax.ShapeDtypeStruct((16, 2, HALF, H), BF16),
            jax.ShapeDtypeStruct((16, 8, 128), F32),
        ),
        in_specs=[smem, vmem, vmem, vmem],
        out_specs=(vmem,) * 3,
        scratch_shapes=[
            pltpu.VMEM((ROWS, H), BF16),
            pltpu.VMEM((8, 128), F32),
            pltpu.VMEM((16, PIECE, H), BF16),
            pltpu.VMEM((2, HALF, H), BF16),
            pltpu.VMEM((2, 2, HALF, H), BF16),
            dma((16,)), dma((16,)),
            dma((1,)), dma((1,)),
            dma((16,)), dma((16,)),
            dma((16,)), dma((2,)),
            dma((16,)), dma((16,)),
            dma((16,)), dma((16,)),
            dma((2, N_GV)), dma((N_GV,)),
            dma((N_GV,)), dma((N_GV,)),
        ],
        compiler_params=pltpu.CompilerParams(
            collective_id=1, has_side_effects=True, vmem_limit_bytes=VMEM_LIMIT
        ),
        name="root_sum",
    )(upw, gv, up_s, up_u)


def down_kernel(
    count_ref, parent_ref, gvs_ref, total_ref, wtiles_ref, mid_gain_ref, mid_value_ref, root_cov_ref,
    up_s, up_u, mid_s, mid_u, leaf_s, leaf_u, sc_ref, cc_ref, nc_ref,
    root_gain_out, root_value_out, up_gain_out, up_value_out, up_cov_out,
    mid_gain_out, mid_value_out, mid_cov_out, leaf_cov_out,
    root_gain_ref, root_value_ref, up_cov_ref, mid_cov_ref, lcov, blocks, work, feed, out_sems,
):
    outs = []

    def emit(src, dst):
        copy = pltpu.make_async_copy(src, dst, out_sems.at[len(outs)])
        copy.start()
        outs.append(copy)

    for s in range(2):
        emit(gvs_ref.at[s, pl.ds(0, NU)], up_gain_out.at[s])
        emit(gvs_ref.at[s, pl.ds(NU, NX)], up_value_out.at[s])
    emit(mid_gain_ref, mid_gain_out)
    emit(mid_value_ref, mid_value_out)
    weight = jnp.sum(wtiles_ref[...], axis=0)
    scale = 1.0 / weight[:1, :1]
    for i in range(6):
        blocks[i] = total_ref[i * H : (i + 1) * H, :].astype(F32) * scale
    riccati(
        lambda i: blocks[i], sc_ref[...], cc_ref[...], root_gain_ref, root_value_ref, work, feed
    )
    emit(root_gain_ref, root_gain_out)
    emit(root_value_ref, root_value_out)
    noise = nc_ref[...]
    root_gain = root_gain_ref[...]
    root_cov = root_cov_ref[...]
    for s in range(2):
        store_cov(up_cov_ref.at[s], propagate(root_cov, root_gain, up_s[s], up_u[s], noise))
        emit(up_cov_ref.at[s], up_cov_out.at[s])
    parent = parent_ref[0]
    store_cov(
        mid_cov_ref,
        propagate(up_cov_ref[parent], gvs_ref[parent, :NU, :], mid_s[0], mid_u[0], noise),
    )
    emit(mid_cov_ref, mid_cov_out)
    live = count_ref[0]
    mid_cov = mid_cov_ref[...]
    mid_gain = mid_gain_ref[...]
    for c in range(LEAF):
        keep = c < live
        result = propagate(mid_cov, mid_gain, leaf_s[c], leaf_u[c], noise)
        store_cov(lcov.at[c], [jnp.where(keep, block, jnp.zeros_like(block)) for block in result])
        emit(lcov.at[c], leaf_cov_out.at[c])
    for out in outs:
        out.wait()


def down(count, parent, *arrays):
    smem = pl.BlockSpec(memory_space=pltpu.SMEM)
    vmem = pl.BlockSpec(memory_space=pltpu.VMEM)
    hbm = pl.BlockSpec(memory_space=pl.ANY)
    return pl.pallas_call(
        down_kernel,
        out_shape=(
            jax.ShapeDtypeStruct((NU, NX), BF16),
            jax.ShapeDtypeStruct((NX, NX), BF16),
            jax.ShapeDtypeStruct((2, NU, NX), BF16),
            jax.ShapeDtypeStruct((2, NX, NX), BF16),
            jax.ShapeDtypeStruct((2, NX, NX), BF16),
            jax.ShapeDtypeStruct((NU, NX), BF16),
            jax.ShapeDtypeStruct((NX, NX), BF16),
            jax.ShapeDtypeStruct((NX, NX), BF16),
            jax.ShapeDtypeStruct((LEAF, NX, NX), BF16),
        ),
        in_specs=[smem, smem] + [vmem] * len(arrays),
        out_specs=(hbm,) * 9,
        scratch_shapes=[
            pltpu.VMEM((NU, NX), BF16),
            pltpu.VMEM((NX, NX), BF16),
            pltpu.VMEM((2, NX, NX), BF16),
            pltpu.VMEM((NX, NX), BF16),
            pltpu.VMEM((LEAF, NX, NX), BF16),
            pltpu.VMEM((6, H, H), F32),
            pltpu.VMEM((H, H), F32),
            pltpu.VMEM((NU, NX), F32),
            pltpu.SemaphoreType.DMA((15,)),
        ],
        compiler_params=pltpu.CompilerParams(vmem_limit_bytes=VMEM_LIMIT),
        name="down_sweep",
    )(count, parent, *arrays)


def local(
    leaf_state_map,
    leaf_input_map,
    leaf_weight,
    leaf_count,
    mid_state_map,
    mid_input_map,
    mid_weight,
    mid_parent,
    up_state_map,
    up_input_map,
    up_weight,
    root_cov,
    state_cost,
    control_cost,
    noise_cov,
):
    sc = state_cost.reshape(1, NX)
    cc = control_cost.reshape(1, NU)
    nc = noise_cov.reshape(1, NX)
    mid_gain, mid_value = lower(
        leaf_count, leaf_state_map, leaf_input_map, leaf_weight.reshape(1, LEAF), sc, cc
    )
    total, weight = gather(mid_parent, mid_weight, mid_value, mid_state_map, mid_input_map)
    gv = upper(total, weight, sc, cc)
    gvs, root_total, wtiles = root_sum(up_weight, gv, up_state_map, up_input_map)
    outs = down(
        leaf_count, mid_parent, gvs, root_total.reshape(ROWS, H), wtiles, mid_gain, mid_value,
        root_cov, up_state_map, up_input_map, mid_state_map, mid_input_map,
        leaf_state_map, leaf_input_map, sc, cc, nc,
    )
    root_gain, root_value, up_gain, up_value, up_cov, mid_gain, mid_value, mid_cov, leaf_cov = outs
    return (
        root_gain,
        root_value,
        up_gain,
        up_value,
        up_cov,
        mid_gain[None],
        mid_value[None],
        mid_cov[None],
        leaf_cov,
    )


def solution(mesh):
    both = P(("row", "col"))
    return jax.shard_map(
        local,
        mesh=mesh,
        in_specs=(
            both, both, both, both, both, both, both, both,
            P("row"), P("row"), P("row"), P(), P(), P(), P(),
        ),
        out_specs=(P(), P(), P("row"), P("row"), P("row"), both, both, both, both),
        check_vma=False,
    )
```

```python
import functools

import jax
import jax.numpy as jnp
from jax import lax
from jax.experimental import pallas as pl
from jax.experimental.pallas import tpu as pltpu
from jax.sharding import PartitionSpec as P

NX = 512
NU = 256
H = 256
LEAF = 4
ROWS = 6 * H
BLOCKS = ((0, 0), (1, 0), (1, 1), (2, 0), (2, 1), (2, 2))
F32 = jnp.float32
BF16 = jnp.bfloat16
MESH = pl.DeviceIdType.MESH
VMEM_LIMIT = 24 * 1024 * 1024
N_CHUNK = 24
CHUNK = ROWS // N_CHUNK
N_GV = 12
GV_ROWS = NX + NU
GV_CHUNK = GV_ROWS // N_GV
PIECE = ROWS // 16
HALF = PIECE // 2
ERROR_TOL = 1e-4
MAX_CONTRACTION = 0.25
MAX_RATIO = 256.0
MAX_REFINE = 8


def mm(a, b):
    return jnp.dot(a, b, preferred_element_type=F32)


def mm_tn(a, b):
    return lax.dot_general(a, b, (((0,), (0,)), ((), ())), preferred_element_type=F32)


def mm_nt(a, b):
    return lax.dot_general(a, b, (((1,), (1,)), ((), ())), preferred_element_type=F32)


def split(a):
    hi = a.astype(BF16)
    return hi, (a - hi.astype(F32)).astype(BF16)


def iota2(shape, dim):
    return lax.broadcasted_iota(jnp.int32, shape, dim)


def eye_mask(n):
    return iota2((n, n), 0) == iota2((n, n), 1)


def to_column(row):
    n = row.shape[1]
    parts = []
    for i in range(n // 128):
        block = jnp.broadcast_to(row[:, i * 128 : (i + 1) * 128], (128, 128))
        parts.append(jnp.sum(jnp.where(eye_mask(128), block, 0.0), axis=1, keepdims=True))
    return jnp.concatenate(parts, axis=0)


def add_diag(block, row):
    return block + jnp.where(eye_mask(block.shape[0]), row, 0.0)


def all_sum(a):
    return jnp.sum(jnp.sum(a, axis=1, keepdims=True), axis=0, keepdims=True)


def riccati(get, state_row, control_row, gain_ref, value_ref, work, feed):
    hess = add_diag(get(5), control_row)
    ba = jnp.concatenate([get(3), get(4)], axis=1)
    eye = eye_mask(H)
    upper = jnp.max(jnp.max(jnp.sum(jnp.abs(hess), axis=1, keepdims=True), axis=0, keepdims=True))
    lower = jnp.minimum(jnp.min(control_row), upper)
    mid = 0.5 * (upper + lower)
    rad = 0.5 * (upper - lower)
    den = 2.0 * mid * mid - rad * rad
    error0 = rad * rad / den
    steps = jnp.int32(0)
    for j in range(16):
        steps += (error0 > 0.1 ** (0.5**j)).astype(jnp.int32)
    h_hi, h_lo = split(hess)
    ba_hi, ba_lo = split(ba)
    work[...] = jnp.where(eye, 4.0 * mid / den, 0.0) - (2.0 / den) * hess

    def newton(_, carry):
        x_hi = work[...].astype(BF16)
        res = jnp.where(eye, 1.0, 0.0) - mm(h_hi, x_hi)
        work[...] = x_hi.astype(F32) + mm(x_hi, res.astype(BF16))
        return carry

    lax.fori_loop(0, steps, newton, 0)
    x_hi = work[...].astype(BF16)
    res = (jnp.where(eye, 1.0, 0.0) - mm(h_hi, x_hi)) - mm(h_lo, x_hi)
    inv, inv_lo = split(x_hi.astype(F32) + mm(x_hi, res.astype(BF16)))
    feed[...] = -(mm(inv, ba_hi) + (mm(inv, ba_lo) + mm(inv_lo, ba_hi)))

    def unconverged(state):
        count, done, _ = state
        return jnp.logical_and(count < MAX_REFINE, done == 0)

    def refine(state):
        count, _, last = state
        f = feed[...]
        f_hi, f_lo = split(f)
        res = ba + (mm(h_hi, f_hi) + (mm(h_hi, f_lo) + mm(h_lo, f_hi)))
        step = mm(inv, res.astype(BF16))
        new = f - step
        feed[...] = new
        size = jnp.sum(step * step)
        norm = jnp.sum(new * new)
        last = jnp.where(count == 0, norm, last)
        small = jnp.logical_and(
            size <= MAX_CONTRACTION**2 * last, size * size <= ERROR_TOL**2 * norm * last
        )
        return count + 1, small.astype(jnp.int32), size

    first = (upper > MAX_RATIO * lower).astype(jnp.int32) * MAX_REFINE
    _, done, _ = lax.while_loop(unconverged, refine, (first, jnp.int32(0), jnp.float32(0.0)))

    @pl.when(done == 0)
    def _():
        work[...] = hess

        def sweep(k, carry):
            a = work[...]
            row = work[pl.ds(k, 1), :]
            here = iota2((H, H), 1) == k
            col = jnp.sum(jnp.where(here, a, 0.0), axis=1, keepdims=True)
            lane_k = iota2((1, H), 1) == k
            sub_k = iota2((H, 1), 0) == k
            pivot = jnp.sum(jnp.where(lane_k, row, 0.0), axis=1, keepdims=True)
            inv_p = 1.0 / pivot
            col0 = jnp.where(sub_k, 0.0, col)
            row1 = jnp.where(lane_k, 1.0, row) * inv_p
            base = jnp.where(jnp.logical_or(here, sub_k), 0.0, a)
            work[...] = jnp.where(sub_k, row1, base - col0 * row1)
            return carry

        lax.fori_loop(0, H, sweep, 0)
        feed[...] = -jnp.dot(
            work[...], ba, preferred_element_type=F32, precision=lax.Precision.HIGHEST
        )

    f = feed[...]
    f_hi, f_lo = split(f)
    gain_ref[...] = f_hi

    def quad(i, j):
        a = slice(i * H, (i + 1) * H)
        b = slice(j * H, (j + 1) * H)
        return mm_tn(ba_hi[:, a], f_hi[:, b]) + (
            mm_tn(ba_hi[:, a], f_lo[:, b]) + mm_tn(ba_lo[:, a], f_hi[:, b])
        )

    value_ref[:H, :H] = add_diag(get(0) + quad(0, 0), state_row[:, :H]).astype(BF16)
    cross = get(1) + quad(1, 0)
    value_ref[H:, :H] = cross.astype(BF16)
    value_ref[:H, H:] = cross.T.astype(BF16)
    value_ref[H:, H:] = add_diag(get(2) + quad(1, 1), state_row[:, H:]).astype(BF16)


def node_term(value_ref, state_ref, input_ref, put):
    value = value_ref[...]
    xs = [state_ref[:, :H], state_ref[:, H:], input_ref[...]]
    ys = [mm(value, x).astype(BF16) for x in xs]
    for i, (a, b) in enumerate(BLOCKS):
        put(i, mm_tn(xs[a], ys[b]))


def propagate(cov, gain, state, inputs, noise_row):
    closed = (state.astype(F32) + mm(inputs, gain)).astype(BF16)
    moved = mm(closed, cov).astype(BF16)
    top = mm_nt(moved[:H], closed[:H])
    cross = mm_nt(moved[H:], closed[:H])
    low = mm_nt(moved[H:], closed[H:])
    return (
        add_diag(top, noise_row[:, :H]).astype(BF16),
        cross.astype(BF16),
        cross.T.astype(BF16),
        add_diag(low, noise_row[:, H:]).astype(BF16),
    )


def store_cov(ref, blocks):
    ref[:H, :H] = blocks[0]
    ref[H:, :H] = blocks[1]
    ref[:H, H:] = blocks[2]
    ref[H:, H:] = blocks[3]


def lane(row, k):
    return jnp.sum(jnp.where(iota2(row.shape, 1) == k, row, 0.0), axis=1, keepdims=True)


def lower_kernel(
    count_ref, leaf_s, leaf_u, leafw_in, sc_in, cc_in,
    gain_ref, value_ref,
    ls, lu, leafw_ref, sc_ref, cc_ref, total, work, feed, sems,
):
    copies = []
    small = []
    for i, (src, dst) in enumerate(((leafw_in, leafw_ref), (sc_in, sc_ref), (cc_in, cc_ref))):
        small.append(pltpu.make_async_copy(src, dst, sems.at[2 * LEAF + i]))
        small[-1].start()
    for c in range(LEAF):
        copies.append(pltpu.make_async_copy(leaf_s.at[c], ls.at[pl.ds(c * NX, NX)], sems.at[2 * c]))
        copies.append(pltpu.make_async_copy(leaf_u.at[c], lu.at[pl.ds(c * NX, NX)], sems.at[2 * c + 1]))
    for copy in copies:
        copy.start()
    for copy in small:
        copy.wait()
    live = count_ref[0]
    weights = leafw_ref[...].astype(F32)
    weights = jnp.where(iota2(weights.shape, 1) < live, weights, 0.0)
    weights = weights / jnp.sum(weights, axis=1, keepdims=True)
    cost = to_column(sc_ref[...])
    for c in range(LEAF):
        copies[2 * c].wait()
        copies[2 * c + 1].wait()
        scale = cost * lane(weights, c)
        rows = slice(c * NX, (c + 1) * NX)
        xs = [ls[rows, :H], ls[rows, H:], lu[rows, :]]
        ss = [(scale * x.astype(F32)).astype(BF16) for x in xs]
        for i, (a, b) in enumerate(BLOCKS):
            part = mm_tn(xs[a], ss[b])
            if c == 0:
                total[i] = part
            else:
                total[i] += part
    riccati(lambda i: total[i], sc_ref[...], cc_ref[...], gain_ref, value_ref, work, feed)


def lower(count, leaf_s, leaf_u, leafw, sc, cc):
    smem = pl.BlockSpec(memory_space=pltpu.SMEM)
    vmem = pl.BlockSpec(memory_space=pltpu.VMEM)
    hbm = pl.BlockSpec(memory_space=pltpu.HBM)
    leaf_s, leaf_u, leafw, sc, cc = [
        pltpu.with_memory_space_constraint(a, pltpu.HBM) for a in (leaf_s, leaf_u, leafw, sc, cc)
    ]
    return pl.pallas_call(
        lower_kernel,
        out_shape=(
            jax.ShapeDtypeStruct((NU, NX), BF16),
            jax.ShapeDtypeStruct((NX, NX), BF16),
        ),
        in_specs=[smem] + [hbm] * 5,
        out_specs=(vmem,) * 2,
        scratch_shapes=[
            pltpu.VMEM((LEAF * NX, NX), BF16),
            pltpu.VMEM((LEAF * NX, NU), BF16),
            pltpu.VMEM((1, LEAF), BF16),
            pltpu.VMEM((1, NX), F32),
            pltpu.VMEM((1, NU), F32),
            pltpu.VMEM((6, H, H), F32),
            pltpu.VMEM((H, H), F32),
            pltpu.VMEM((NU, NX), F32),
            pltpu.SemaphoreType.DMA((2 * LEAF + 3,)),
        ],
        compiler_params=pltpu.CompilerParams(vmem_limit_bytes=VMEM_LIMIT),
        cost_estimate=pl.CostEstimate(
            flops=LEAF * NX * 2 * (NX + NU) ** 2, bytes_accessed=LEAF * NX * (NX + NU) * 2, transcendentals=0
        ),
        name="lower_nodes",
    )(count, leaf_s, leaf_u, leafw, sc, cc)


def gather_kernel(
    parent_ref, midw_ref, value_ref, mid_s, mid_u,
    total_ref, weight_ref,
    own_buf, other_buf, sib_buf, in_buf, out_buf, tile, sib_tile, in_tile, out_tile,
    sib_send, sib_recv, send_sem, recv_sem,
):
    row = lax.axis_index("row")
    col = lax.axis_index("col")
    z = col // 2
    core = lax.rem(col, 2)
    sibling = col + 1 - 2 * core
    dist = lax.rem(z + 8 - 4 * core, 8)
    is_target = dist == 0
    down = jnp.logical_and(dist >= 1, dist <= 4)
    up_col = 2 * lax.rem(z + 1, 8) + core
    down_col = 2 * lax.rem(z + 7, 8) + core
    next_col = jnp.where(down, down_col, up_col)
    side = jnp.where(dist == 7, 1, 0)
    has_up = jnp.logical_and(dist != 4, dist != 5)

    barrier = pltpu.get_barrier_semaphore()
    for peer in (sibling, up_col, down_col):
        pl.semaphore_signal(barrier, inc=1, device_id=(row, peer), device_id_type=MESH)
    weight = midw_ref[0]
    parent = parent_ref[0]
    w_own = jnp.where(parent == core, weight, 0.0)
    w_other = jnp.where(parent == core, 0.0, weight)

    def put(i, block):
        own_buf[i * H : (i + 1) * H, :] = w_own * block
        other_buf[i * H : (i + 1) * H, :] = (w_other * block).astype(BF16)

    node_term(value_ref, mid_s.at[0], mid_u.at[0], put)
    tile[...] = jnp.where(iota2((8, 128), 0) == parent, weight, 0.0)
    pl.semaphore_wait(barrier, 3)

    def chunk(c):
        return pl.ds(pl.multiple_of(c * CHUNK, 16), CHUNK)

    def remote(src, dst, send, recv, peer):
        return pltpu.make_async_remote_copy(
            src_ref=src, dst_ref=dst, send_sem=send, recv_sem=recv,
            device_id=(row, peer), device_id_type=MESH,
        )

    def sib_copy(c):
        return remote(
            other_buf.at[chunk(c)], sib_buf.at[chunk(c)], sib_send.at[c], sib_recv.at[c], sibling
        )

    def chain_copy(c, to_side):
        return remote(
            out_buf.at[chunk(c)], in_buf.at[to_side, chunk(c)],
            send_sem.at[c], recv_sem.at[to_side, c], next_col,
        )

    def sib_tile_copy():
        return remote(tile, sib_tile, sib_send.at[N_CHUNK], sib_recv.at[N_CHUNK], sibling)

    def tile_copy(to_side):
        return remote(
            out_tile, in_tile.at[to_side],
            send_sem.at[N_CHUNK], recv_sem.at[to_side, N_CHUNK], next_col,
        )

    def start_sib(c, carry):
        sib_copy(c).start()
        return carry

    lax.fori_loop(0, N_CHUNK, start_sib, 0)
    sib_tile_copy().start()

    def step(c, carry):
        rows = chunk(c)
        sib_copy(c).wait_recv()
        part = own_buf[rows, :] + sib_buf[rows, :].astype(F32)

        @pl.when(jnp.logical_not(has_up))
        def _():
            out_buf[rows, :] = part.astype(BF16)
            chain_copy(c, side).start()

        @pl.when(has_up)
        def _():
            chain_copy(c, 0).wait_recv()
            more = part + in_buf[0, rows, :].astype(F32)

            @pl.when(is_target)
            def _():
                chain_copy(c, 1).wait_recv()
                total_ref[rows, :] = more + in_buf[1, rows, :].astype(F32)

            @pl.when(jnp.logical_not(is_target))
            def _():
                out_buf[rows, :] = more.astype(BF16)
                chain_copy(c, side).start()

        return carry

    lax.fori_loop(0, N_CHUNK, step, 0)
    sib_tile_copy().wait_recv()
    tiles = tile[...] + sib_tile[...]

    @pl.when(jnp.logical_not(has_up))
    def _():
        out_tile[...] = tiles
        tile_copy(side).start()

    @pl.when(has_up)
    def _():
        tile_copy(0).wait_recv()
        more = tiles + in_tile[0]

        @pl.when(is_target)
        def _():
            tile_copy(1).wait_recv()
            weight_ref[...] = more + in_tile[1]

        @pl.when(jnp.logical_not(is_target))
        def _():
            out_tile[...] = more
            tile_copy(side).start()

    def drain(c, carry):
        sib_copy(c).wait_send()

        @pl.when(jnp.logical_not(is_target))
        def _():
            chain_copy(c, side).wait_send()

        return carry

    lax.fori_loop(0, N_CHUNK, drain, 0)
    sib_tile_copy().wait_send()

    @pl.when(jnp.logical_not(is_target))
    def _():
        tile_copy(side).wait_send()


def gather(parent, midw, value, mid_s, mid_u):
    smem = pl.BlockSpec(memory_space=pltpu.SMEM)
    vmem = pl.BlockSpec(memory_space=pltpu.VMEM)
    dma = pltpu.SemaphoreType.DMA
    return pl.pallas_call(
        gather_kernel,
        out_shape=(
            jax.ShapeDtypeStruct((ROWS, H), F32),
            jax.ShapeDtypeStruct((8, 128), F32),
        ),
        in_specs=[smem, smem, vmem, vmem, vmem],
        out_specs=(vmem,) * 2,
        scratch_shapes=[
            pltpu.VMEM((ROWS, H), F32),
            pltpu.VMEM((ROWS, H), BF16),
            pltpu.VMEM((ROWS, H), BF16),
            pltpu.VMEM((2, ROWS, H), BF16),
            pltpu.VMEM((ROWS, H), BF16),
            pltpu.VMEM((8, 128), F32),
            pltpu.VMEM((8, 128), F32),
            pltpu.VMEM((2, 8, 128), F32),
            pltpu.VMEM((8, 128), F32),
            dma((N_CHUNK + 1,)),
            dma((N_CHUNK + 1,)),
            dma((N_CHUNK + 1,)),
            dma((2, N_CHUNK + 1)),
        ],
        compiler_params=pltpu.CompilerParams(
            collective_id=0, has_side_effects=True, vmem_limit_bytes=VMEM_LIMIT
        ),
        name="group_sum",
    )(parent, midw, value, mid_s, mid_u)


def upper_kernel(total_ref, weight_ref, sc_ref, cc_ref, gv_ref, blocks, work, feed):
    col = lax.axis_index("col")
    core = lax.rem(col, 2)

    @pl.when(col == 9 * core)
    def _():
        picked = jnp.where(iota2((8, 128), 0) == core, weight_ref[...], 0.0)
        scale = 1.0 / jnp.sum(picked, axis=0, keepdims=True)[:, :1]
        for i in range(6):
            blocks[i] = total_ref[i * H : (i + 1) * H, :] * scale
        gain_ref = gv_ref.at[pl.ds(0, NU)]
        value_ref = gv_ref.at[pl.ds(NU, NX)]
        riccati(lambda i: blocks[i], sc_ref[...], cc_ref[...], gain_ref, value_ref, work, feed)


def upper(total, weight, sc, cc):
    vmem = pl.BlockSpec(memory_space=pltpu.VMEM)
    return pl.pallas_call(
        upper_kernel,
        out_shape=jax.ShapeDtypeStruct((GV_ROWS, NX), BF16),
        in_specs=[vmem] * 4,
        out_specs=vmem,
        scratch_shapes=[
            pltpu.VMEM((6, H, H), F32),
            pltpu.VMEM((H, H), F32),
            pltpu.VMEM((NU, NX), F32),
        ],
        compiler_params=pltpu.CompilerParams(vmem_limit_bytes=VMEM_LIMIT),
        name="upper_nodes",
    )(total, weight, sc, cc)


def hops(step):
    return min(step, 4 - step)


NEAR = sorted(
    [(dy, dx) for dy in range(4) for dx in range(4) if dy or dx],
    key=lambda step: hops(step[0]) + hops(step[1]),
)


def root_kernel(
    upw_ref, gv_ref, up_s, up_u, gvs_ref, total_ref, wtiles_ref,
    term_ref, wtile_ref, in_buf, piece_buf, pair_buf,
    w_send, w_recv, ws_send, ws_recv, a_send, a_recv, b_send, b_recv, c_send, c_recv,
    s_send, s_recv, g_send, g_recv, gs_send, gs_recv,
):
    row = lax.axis_index("row")
    col = lax.axis_index("col")
    z = col // 2
    core = lax.rem(col, 2)
    sibling = col + 1 - 2 * core
    dist = lax.rem(z + 8 - 4 * core, 8)
    is_target = dist == 0
    is_adder = dist == 4
    is_plain = jnp.logical_not(jnp.logical_or(is_target, is_adder))
    up_col = 2 * lax.rem(z + 1, 8) + core
    down_col = 2 * lax.rem(z + 7, 8) + core
    other_adder = 2 * lax.rem(z + 4, 8) + 1 - core
    slot = 1 - core
    barrier = pltpu.get_barrier_semaphore()

    def signal(to_row, to_col):
        pl.semaphore_signal(barrier, inc=1, device_id=(to_row, to_col), device_id_type=MESH)

    def peers(body):
        def one(k, carry):
            body(lax.rem(row + k, 16))
            return carry

        lax.fori_loop(1, 16, one, 0)

    def at_step(step):
        return lax.rem(row // 4 + step[0], 4) * 4 + lax.rem(lax.rem(row, 4) + step[1], 4)

    def far_first(body):
        for step in reversed(NEAR):
            body(at_step(step))

    def near_first(body):
        for step in NEAR:
            body(at_step(step))

    for to_col in (sibling, up_col, down_col):
        signal(row, to_col)

    @pl.when(is_target)
    def _():
        peers(lambda p: signal(p, sibling))

    @pl.when(is_adder)
    def _():
        peers(lambda p: signal(p, sibling))
        peers(lambda p: signal(p, col))
        signal(row, other_adder)
        for off in (1, 2, 3, 5, 6, 7):
            for half in range(2):
                signal(row, 2 * lax.rem(z + off, 8) + half)

    @pl.when(is_plain)
    def _():
        peers(lambda p: signal(p, col))
        signal(row, 1)
        signal(row, 8)

    def remote(src, dst, send, recv, to_row, to_col):
        return pltpu.make_async_remote_copy(
            src_ref=src, dst_ref=dst, send_sem=send, recv_sem=recv,
            device_id=(to_row, to_col), device_id_type=MESH,
        )

    def a_copy(to_row, at):
        return remote(
            term_ref.at[pl.ds(pl.multiple_of(to_row * PIECE, 16), PIECE)], in_buf.at[at],
            a_send.at[to_row], a_recv.at[at], to_row, sibling,
        )

    def b_half(off, half, of_slot):
        return remote(
            piece_buf.at[half], pair_buf.at[of_slot, half],
            b_send.at[2 * off + half], b_recv.at[of_slot], row, 2 * lax.rem(z + off, 8) + half,
        )

    def b_whole(of_slot):
        return remote(
            piece_buf, pair_buf.at[of_slot], b_send.at[0], b_recv.at[of_slot], row, other_adder
        )

    def c_half(to_row, at):
        part = total_ref.at[at, core]
        return remote(part, part, c_send.at[to_row], c_recv.at[at], to_row, col)

    def c_whole(to_row, at):
        part = total_ref.at[at]
        return remote(part, part, c_send.at[to_row], c_recv.at[at], to_row, col)

    def s_half(at, half):
        part = total_ref.at[at, half]
        return remote(part, part, s_send.at[at], s_recv.at[at], row, sibling)

    def s_whole(at):
        part = total_ref.at[at]
        return remote(part, part, s_send.at[at], s_recv.at[at], row, sibling)

    def w_copy(to_row, at):
        return remote(wtile_ref, wtiles_ref.at[at], w_send.at[to_row], w_recv.at[at], to_row, col)

    def ws_copy():
        return remote(wtiles_ref, wtiles_ref, ws_send.at[0], ws_recv.at[0], row, sibling)

    def g_part(c, of_slot):
        return gvs_ref.at[of_slot, pl.ds(pl.multiple_of(c * GV_CHUNK, 16), GV_CHUNK)]

    def g_copy(c, to_col, way):
        part = g_part(c, core)
        return remote(part, part, g_send.at[way, c], g_recv.at[c], row, to_col)

    def gs_copy(c, of_slot):
        part = g_part(c, of_slot)
        return remote(part, part, gs_send.at[c], gs_recv.at[c], row, sibling)

    def gv_chunks(body, first=0, last=N_GV):
        def one(c, carry):
            body(c)
            return carry

        lax.fori_loop(first, last, one, 0)

    to_up = dist <= 3
    to_down = jnp.logical_or(dist == 0, dist >= 6)

    def forward(c):
        @pl.when(to_up)
        def _():
            g_copy(c, up_col, 0).start()

        @pl.when(to_down)
        def _():
            g_copy(c, down_col, 1).start()

        gs_copy(c, core).start()

    def relay(c):
        g_copy(c, up_col, 0).wait_recv()
        forward(c)

    def pieces(body):
        def one(at, carry):
            body(at)
            return carry

        lax.fori_loop(0, 16, one, 0)

    def send_tiles():
        peers(lambda p: w_copy(p, row).start())
        wtiles_ref[pl.ds(row, 1)] = wtile_ref[...][None]

    wtile_ref[...] = jnp.full((8, 128), upw_ref[0] + upw_ref[1], F32)

    @pl.when(is_target)
    def _():
        gvs_ref[pl.ds(core, 1)] = gv_ref[...][None]
        up_weight = jnp.where(core == 0, upw_ref[0], upw_ref[1])
        pl.semaphore_wait(barrier, 18)
        gv_chunks(forward)

        def put(i, block):
            term_ref[i * H : (i + 1) * H, :] = (up_weight * block).astype(BF16)

        node_term(gv_ref.at[pl.ds(NU, NX)], up_s.at[core], up_u.at[core], put)
        far_first(lambda p: a_copy(p, row).start())
        a_copy(row, row).start()

    @pl.when(is_adder)
    def _():
        pl.semaphore_wait(barrier, 46)

    @pl.when(is_plain)
    def _():
        pl.semaphore_wait(barrier, 20)

    @pl.when(is_target)
    def _():
        pieces(lambda at: s_whole(at).wait_recv())
        ws_copy().wait_recv()
        pieces(lambda p: a_copy(p, row).wait_send())

    @pl.when(is_adder)
    def _():
        send_tiles()
        a_copy(row, row).wait_recv()
        acc = in_buf[row].astype(F32)
        for step in NEAR:
            source = at_step(step)
            a_copy(source, source).wait_recv()
            acc = acc + in_buf[source].astype(F32)
        piece = acc.astype(BF16)
        piece_buf[0] = piece[:HALF]
        piece_buf[1] = piece[HALF:]
        b_whole(slot).start()
        for off in (3, 5, 2, 6, 1, 7):
            for half in range(2):
                b_half(off, half, slot).start()
        own = piece_buf[...].astype(F32)
        b_whole(core).wait_recv()
        pair = own + pair_buf[core].astype(F32)
        total_ref[pl.ds(row, 1)] = pair.astype(BF16)[None]
        far_first(lambda p: c_whole(p, row).start())
        s_whole(row).start()
        def relay_piece(p):
            c_whole(p, p).wait_recv()
            s_whole(p).start()

        near_first(relay_piece)
        gv_chunks(relay)
        peers(lambda p: w_copy(p, p).wait_recv())
        ws_copy().start()
        ws_copy().wait_send()
        pieces(lambda at: s_whole(at).wait_send())
        peers(lambda p: c_whole(p, row).wait_send())
        peers(lambda p: w_copy(p, row).wait_send())
        b_whole(slot).wait_send()
        for off in (3, 5, 2, 6, 1, 7):
            for half in range(2):
                b_half(off, half, slot).wait_send()

    steps = jnp.minimum(dist, 8 - dist)
    early = jnp.where(steps <= 2, N_GV, N_GV // 2)

    @pl.when(is_plain)
    def _():
        send_tiles()
        gv_chunks(relay, 0, early)
        b_half(1, core, 0).wait_recv()
        b_half(1, core, 1).wait_recv()
        pair = pair_buf[0, core].astype(F32) + pair_buf[1, core].astype(F32)
        total_ref[pl.ds(row, 1), pl.ds(core, 1)] = pair.astype(BF16)[None, None]
        far_first(lambda p: c_half(p, row).start())
        s_half(row, core).start()
        gv_chunks(relay, early, N_GV)

        def relay_piece(p):
            c_half(p, p).wait_recv()
            s_half(p, core).start()

        near_first(relay_piece)

        def finish(at):
            s_half(at, 1 - core).wait_recv()
            s_half(at, core).wait_send()

        pieces(finish)
        peers(lambda p: w_copy(p, p).wait_recv())
        peers(lambda p: c_half(p, row).wait_send())
        peers(lambda p: w_copy(p, row).wait_send())

    def finish_gv(c):
        gs_copy(c, 1 - core).wait_recv()
        gs_copy(c, core).wait_send()

        @pl.when(to_up)
        def _():
            g_copy(c, up_col, 0).wait_send()

        @pl.when(to_down)
        def _():
            g_copy(c, down_col, 1).wait_send()

    gv_chunks(finish_gv)


def root_sum(upw, gv, up_s, up_u):
    smem = pl.BlockSpec(memory_space=pltpu.SMEM)
    vmem = pl.BlockSpec(memory_space=pltpu.VMEM)
    dma = pltpu.SemaphoreType.DMA
    return pl.pallas_call(
        root_kernel,
        out_shape=(
            jax.ShapeDtypeStruct((2, GV_ROWS, NX), BF16),
            jax.ShapeDtypeStruct((16, 2, HALF, H), BF16),
            jax.ShapeDtypeStruct((16, 8, 128), F32),
        ),
        in_specs=[smem, vmem, vmem, vmem],
        out_specs=(vmem,) * 3,
        scratch_shapes=[
            pltpu.VMEM((ROWS, H), BF16),
            pltpu.VMEM((8, 128), F32),
            pltpu.VMEM((16, PIECE, H), BF16),
            pltpu.VMEM((2, HALF, H), BF16),
            pltpu.VMEM((2, 2, HALF, H), BF16),
            dma((16,)), dma((16,)),
            dma((1,)), dma((1,)),
            dma((16,)), dma((16,)),
            dma((16,)), dma((2,)),
            dma((16,)), dma((16,)),
            dma((16,)), dma((16,)),
            dma((2, N_GV)), dma((N_GV,)),
            dma((N_GV,)), dma((N_GV,)),
        ],
        compiler_params=pltpu.CompilerParams(
            collective_id=1, has_side_effects=True, vmem_limit_bytes=VMEM_LIMIT
        ),
        name="root_sum",
    )(upw, gv, up_s, up_u)


def down_kernel(
    count_ref, parent_ref, gvs_ref, total_ref, wtiles_ref, mid_gain_ref, mid_value_ref, root_cov_ref,
    up_s, up_u, mid_s, mid_u, leaf_s, leaf_u, sc_ref, cc_ref, nc_ref,
    root_gain_out, root_value_out, up_gain_out, up_value_out, up_cov_out,
    mid_gain_out, mid_value_out, mid_cov_out, leaf_cov_out,
    root_gain_ref, root_value_ref, up_cov_ref, mid_cov_ref, lcov, blocks, work, feed, out_sems,
):
    outs = []

    def emit(src, dst):
        copy = pltpu.make_async_copy(src, dst, out_sems.at[len(outs)])
        copy.start()
        outs.append(copy)

    for s in range(2):
        emit(gvs_ref.at[s, pl.ds(0, NU)], up_gain_out.at[s])
        emit(gvs_ref.at[s, pl.ds(NU, NX)], up_value_out.at[s])
    emit(mid_gain_ref, mid_gain_out)
    emit(mid_value_ref, mid_value_out)
    weight = jnp.sum(wtiles_ref[...], axis=0)
    scale = 1.0 / weight[:1, :1]
    for i in range(6):
        blocks[i] = total_ref[i * H : (i + 1) * H, :].astype(F32) * scale
    riccati(
        lambda i: blocks[i], sc_ref[...], cc_ref[...], root_gain_ref, root_value_ref, work, feed
    )
    emit(root_gain_ref, root_gain_out)
    emit(root_value_ref, root_value_out)
    noise = nc_ref[...]
    root_gain = root_gain_ref[...]
    root_cov = root_cov_ref[...]
    for s in range(2):
        store_cov(up_cov_ref.at[s], propagate(root_cov, root_gain, up_s[s], up_u[s], noise))
        emit(up_cov_ref.at[s], up_cov_out.at[s])
    parent = parent_ref[0]
    store_cov(
        mid_cov_ref,
        propagate(up_cov_ref[parent], gvs_ref[parent, :NU, :], mid_s[0], mid_u[0], noise),
    )
    emit(mid_cov_ref, mid_cov_out)
    live = count_ref[0]
    mid_cov = mid_cov_ref[...]
    mid_gain = mid_gain_ref[...]
    for c in range(LEAF):
        keep = c < live
        result = propagate(mid_cov, mid_gain, leaf_s[c], leaf_u[c], noise)
        store_cov(lcov.at[c], [jnp.where(keep, block, jnp.zeros_like(block)) for block in result])
        emit(lcov.at[c], leaf_cov_out.at[c])
    for out in outs:
        out.wait()


def down(count, parent, *arrays):
    smem = pl.BlockSpec(memory_space=pltpu.SMEM)
    vmem = pl.BlockSpec(memory_space=pltpu.VMEM)
    hbm = pl.BlockSpec(memory_space=pl.ANY)
    return pl.pallas_call(
        down_kernel,
        out_shape=(
            jax.ShapeDtypeStruct((NU, NX), BF16),
            jax.ShapeDtypeStruct((NX, NX), BF16),
            jax.ShapeDtypeStruct((2, NU, NX), BF16),
            jax.ShapeDtypeStruct((2, NX, NX), BF16),
            jax.ShapeDtypeStruct((2, NX, NX), BF16),
            jax.ShapeDtypeStruct((NU, NX), BF16),
            jax.ShapeDtypeStruct((NX, NX), BF16),
            jax.ShapeDtypeStruct((NX, NX), BF16),
            jax.ShapeDtypeStruct((LEAF, NX, NX), BF16),
        ),
        in_specs=[smem, smem] + [vmem] * len(arrays),
        out_specs=(hbm,) * 9,
        scratch_shapes=[
            pltpu.VMEM((NU, NX), BF16),
            pltpu.VMEM((NX, NX), BF16),
            pltpu.VMEM((2, NX, NX), BF16),
            pltpu.VMEM((NX, NX), BF16),
            pltpu.VMEM((LEAF, NX, NX), BF16),
            pltpu.VMEM((6, H, H), F32),
            pltpu.VMEM((H, H), F32),
            pltpu.VMEM((NU, NX), F32),
            pltpu.SemaphoreType.DMA((15,)),
        ],
        compiler_params=pltpu.CompilerParams(vmem_limit_bytes=VMEM_LIMIT),
        name="down_sweep",
    )(count, parent, *arrays)


def local(
    leaf_state_map,
    leaf_input_map,
    leaf_weight,
    leaf_count,
    mid_state_map,
    mid_input_map,
    mid_weight,
    mid_parent,
    up_state_map,
    up_input_map,
    up_weight,
    root_cov,
    state_cost,
    control_cost,
    noise_cov,
):
    sc = state_cost.reshape(1, NX)
    cc = control_cost.reshape(1, NU)
    nc = noise_cov.reshape(1, NX)
    mid_gain, mid_value = lower(
        leaf_count, leaf_state_map, leaf_input_map, leaf_weight.reshape(1, LEAF), sc, cc
    )
    total, weight = gather(mid_parent, mid_weight, mid_value, mid_state_map, mid_input_map)
    gv = upper(total, weight, sc, cc)
    gvs, root_total, wtiles = root_sum(up_weight, gv, up_state_map, up_input_map)
    outs = down(
        leaf_count, mid_parent, gvs, root_total.reshape(ROWS, H), wtiles, mid_gain, mid_value,
        root_cov, up_state_map, up_input_map, mid_state_map, mid_input_map,
        leaf_state_map, leaf_input_map, sc, cc, nc,
    )
    root_gain, root_value, up_gain, up_value, up_cov, mid_gain, mid_value, mid_cov, leaf_cov = outs
    return (
        root_gain,
        root_value,
        up_gain,
        up_value,
        up_cov,
        mid_gain[None],
        mid_value[None],
        mid_cov[None],
        leaf_cov,
    )


def solution(mesh):
    both = P(("row", "col"))
    return jax.shard_map(
        local,
        mesh=mesh,
        in_specs=(
            both, both, both, both, both, both, both, both,
            P("row"), P("row"), P("row"), P(), P(), P(), P(),
        ),
        out_specs=(P(), P(), P("row"), P("row"), P("row"), both, both, both, both),
        check_vma=False,
    )
```

```python
import functools

import jax
import jax.numpy as jnp
from jax import lax
from jax.experimental import pallas as pl
from jax.experimental.pallas import tpu as pltpu
from jax.sharding import PartitionSpec as P

NX = 512
NU = 256
H = 256
LEAF = 4
ROWS = 6 * H
BLOCKS = ((0, 0), (1, 0), (1, 1), (2, 0), (2, 1), (2, 2))
F32 = jnp.float32
BF16 = jnp.bfloat16
MESH = pl.DeviceIdType.MESH
VMEM_LIMIT = 24 * 1024 * 1024
N_CHUNK = 24
CHUNK = ROWS // N_CHUNK
N_GV = 12
GV_ROWS = NX + NU
GV_CHUNK = GV_ROWS // N_GV
PIECE = ROWS // 16
HALF = PIECE // 2
ERROR_TOL = 1e-4
MAX_CONTRACTION = 0.25
MAX_RATIO = 256.0
MAX_REFINE = 8


def mm(a, b):
    return jnp.dot(a, b, preferred_element_type=F32)


def mm_tn(a, b):
    return lax.dot_general(a, b, (((0,), (0,)), ((), ())), preferred_element_type=F32)


def mm_nt(a, b):
    return lax.dot_general(a, b, (((1,), (1,)), ((), ())), preferred_element_type=F32)


def split(a):
    hi = a.astype(BF16)
    return hi, (a - hi.astype(F32)).astype(BF16)


def iota2(shape, dim):
    return lax.broadcasted_iota(jnp.int32, shape, dim)


def eye_mask(n):
    return iota2((n, n), 0) == iota2((n, n), 1)


def to_column(row):
    n = row.shape[1]
    parts = []
    for i in range(n // 128):
        block = jnp.broadcast_to(row[:, i * 128 : (i + 1) * 128], (128, 128))
        parts.append(jnp.sum(jnp.where(eye_mask(128), block, 0.0), axis=1, keepdims=True))
    return jnp.concatenate(parts, axis=0)


def add_diag(block, row):
    return block + jnp.where(eye_mask(block.shape[0]), row, 0.0)


def all_sum(a):
    return jnp.sum(jnp.sum(a, axis=1, keepdims=True), axis=0, keepdims=True)


def riccati(get, state_row, control_row, gain_ref, value_ref, work, feed):
    hess = add_diag(get(5), control_row)
    ba = jnp.concatenate([get(3), get(4)], axis=1)
    eye = eye_mask(H)
    upper = jnp.max(jnp.max(jnp.sum(jnp.abs(hess), axis=1, keepdims=True), axis=0, keepdims=True))
    lower = jnp.minimum(jnp.min(control_row), upper)
    mid = 0.5 * (upper + lower)
    rad = 0.5 * (upper - lower)
    den = 2.0 * mid * mid - rad * rad
    error0 = rad * rad / den
    steps = jnp.int32(0)
    for j in range(16):
        steps += (error0 > 0.3 ** (0.5**j)).astype(jnp.int32)
    h_hi, h_lo = split(hess)
    ba_hi, ba_lo = split(ba)
    work[...] = jnp.where(eye, 4.0 * mid / den, 0.0) - (2.0 / den) * hess

    def newton(_, carry):
        x_hi = work[...].astype(BF16)
        res = jnp.where(eye, 1.0, 0.0) - mm(h_hi, x_hi)
        work[...] = x_hi.astype(F32) + mm(x_hi, res.astype(BF16))
        return carry

    lax.fori_loop(0, steps, newton, 0)
    x_hi = work[...].astype(BF16)
    res = (jnp.where(eye, 1.0, 0.0) - mm(h_hi, x_hi)) - mm(h_lo, x_hi)
    inv, inv_lo = split(x_hi.astype(F32) + mm(x_hi, res.astype(BF16)))
    feed[...] = -(mm(inv, ba_hi) + (mm(inv, ba_lo) + mm(inv_lo, ba_hi)))

    def unconverged(state):
        count, done, _ = state
        return jnp.logical_and(count < MAX_REFINE, done == 0)

    def refine(state):
        count, _, last = state
        f = feed[...]
        f_hi, f_lo = split(f)
        res = ba + (mm(h_hi, f_hi) + (mm(h_hi, f_lo) + mm(h_lo, f_hi)))
        step = mm(inv, res.astype(BF16))
        new = f - step
        feed[...] = new
        size = jnp.sum(step * step)
        norm = jnp.sum(new * new)
        last = jnp.where(count == 0, norm, last)
        small = jnp.logical_and(
            size <= MAX_CONTRACTION**2 * last, size * size <= ERROR_TOL**2 * norm * last
        )
        return count + 1, small.astype(jnp.int32), size

    first = (upper > MAX_RATIO * lower).astype(jnp.int32) * MAX_REFINE
    _, done, _ = lax.while_loop(unconverged, refine, (first, jnp.int32(0), jnp.float32(0.0)))

    @pl.when(done == 0)
    def _():
        work[...] = hess

        def sweep(k, carry):
            a = work[...]
            row = work[pl.ds(k, 1), :]
            here = iota2((H, H), 1) == k
            col = jnp.sum(jnp.where(here, a, 0.0), axis=1, keepdims=True)
            lane_k = iota2((1, H), 1) == k
            sub_k = iota2((H, 1), 0) == k
            pivot = jnp.sum(jnp.where(lane_k, row, 0.0), axis=1, keepdims=True)
            inv_p = 1.0 / pivot
            col0 = jnp.where(sub_k, 0.0, col)
            row1 = jnp.where(lane_k, 1.0, row) * inv_p
            base = jnp.where(jnp.logical_or(here, sub_k), 0.0, a)
            work[...] = jnp.where(sub_k, row1, base - col0 * row1)
            return carry

        lax.fori_loop(0, H, sweep, 0)
        feed[...] = -jnp.dot(
            work[...], ba, preferred_element_type=F32, precision=lax.Precision.HIGHEST
        )

    f = feed[...]
    f_hi, f_lo = split(f)
    gain_ref[...] = f_hi

    def quad(i, j):
        a = slice(i * H, (i + 1) * H)
        b = slice(j * H, (j + 1) * H)
        return mm_tn(ba_hi[:, a], f_hi[:, b]) + (
            mm_tn(ba_hi[:, a], f_lo[:, b]) + mm_tn(ba_lo[:, a], f_hi[:, b])
        )

    value_ref[:H, :H] = add_diag(get(0) + quad(0, 0), state_row[:, :H]).astype(BF16)
    cross = get(1) + quad(1, 0)
    value_ref[H:, :H] = cross.astype(BF16)
    value_ref[:H, H:] = cross.T.astype(BF16)
    value_ref[H:, H:] = add_diag(get(2) + quad(1, 1), state_row[:, H:]).astype(BF16)


def node_term(value_ref, state_ref, input_ref, put):
    value = value_ref[...]
    xs = [state_ref[:, :H], state_ref[:, H:], input_ref[...]]
    ys = [mm(value, x).astype(BF16) for x in xs]
    for i, (a, b) in enumerate(BLOCKS):
        put(i, mm_tn(xs[a], ys[b]))


def propagate(cov, gain, state, inputs, noise_row):
    closed = (state.astype(F32) + mm(inputs, gain)).astype(BF16)
    moved = mm(closed, cov).astype(BF16)
    top = mm_nt(moved[:H], closed[:H])
    cross = mm_nt(moved[H:], closed[:H])
    low = mm_nt(moved[H:], closed[H:])
    return (
        add_diag(top, noise_row[:, :H]).astype(BF16),
        cross.astype(BF16),
        cross.T.astype(BF16),
        add_diag(low, noise_row[:, H:]).astype(BF16),
    )


def store_cov(ref, blocks):
    ref[:H, :H] = blocks[0]
    ref[H:, :H] = blocks[1]
    ref[:H, H:] = blocks[2]
    ref[H:, H:] = blocks[3]


def lane(row, k):
    return jnp.sum(jnp.where(iota2(row.shape, 1) == k, row, 0.0), axis=1, keepdims=True)


def lower_kernel(
    count_ref, leaf_s, leaf_u, leafw_in, sc_in, cc_in,
    gain_ref, value_ref,
    ls, lu, leafw_ref, sc_ref, cc_ref, total, work, feed, sems,
):
    copies = []
    small = []
    for i, (src, dst) in enumerate(((leafw_in, leafw_ref), (sc_in, sc_ref), (cc_in, cc_ref))):
        small.append(pltpu.make_async_copy(src, dst, sems.at[2 * LEAF + i]))
        small[-1].start()
    for c in range(LEAF):
        copies.append(pltpu.make_async_copy(leaf_s.at[c], ls.at[pl.ds(c * NX, NX)], sems.at[2 * c]))
        copies.append(pltpu.make_async_copy(leaf_u.at[c], lu.at[pl.ds(c * NX, NX)], sems.at[2 * c + 1]))
    for copy in copies:
        copy.start()
    for copy in small:
        copy.wait()
    live = count_ref[0]
    weights = leafw_ref[...].astype(F32)
    weights = jnp.where(iota2(weights.shape, 1) < live, weights, 0.0)
    weights = weights / jnp.sum(weights, axis=1, keepdims=True)
    cost = to_column(sc_ref[...])
    for c in range(LEAF):
        copies[2 * c].wait()
        copies[2 * c + 1].wait()
        scale = cost * lane(weights, c)
        rows = slice(c * NX, (c + 1) * NX)
        xs = [ls[rows, :H], ls[rows, H:], lu[rows, :]]
        ss = [(scale * x.astype(F32)).astype(BF16) for x in xs]
        for i, (a, b) in enumerate(BLOCKS):
            part = mm_tn(xs[a], ss[b])
            if c == 0:
                total[i] = part
            else:
                total[i] += part
    riccati(lambda i: total[i], sc_ref[...], cc_ref[...], gain_ref, value_ref, work, feed)


def lower(count, leaf_s, leaf_u, leafw, sc, cc):
    smem = pl.BlockSpec(memory_space=pltpu.SMEM)
    vmem = pl.BlockSpec(memory_space=pltpu.VMEM)
    hbm = pl.BlockSpec(memory_space=pltpu.HBM)
    leaf_s, leaf_u, leafw, sc, cc = [
        pltpu.with_memory_space_constraint(a, pltpu.HBM) for a in (leaf_s, leaf_u, leafw, sc, cc)
    ]
    return pl.pallas_call(
        lower_kernel,
        out_shape=(
            jax.ShapeDtypeStruct((NU, NX), BF16),
            jax.ShapeDtypeStruct((NX, NX), BF16),
        ),
        in_specs=[smem] + [hbm] * 5,
        out_specs=(vmem,) * 2,
        scratch_shapes=[
            pltpu.VMEM((LEAF * NX, NX), BF16),
            pltpu.VMEM((LEAF * NX, NU), BF16),
            pltpu.VMEM((1, LEAF), BF16),
            pltpu.VMEM((1, NX), F32),
            pltpu.VMEM((1, NU), F32),
            pltpu.VMEM((6, H, H), F32),
            pltpu.VMEM((H, H), F32),
            pltpu.VMEM((NU, NX), F32),
            pltpu.SemaphoreType.DMA((2 * LEAF + 3,)),
        ],
        compiler_params=pltpu.CompilerParams(vmem_limit_bytes=VMEM_LIMIT),
        cost_estimate=pl.CostEstimate(
            flops=LEAF * NX * 2 * (NX + NU) ** 2, bytes_accessed=LEAF * NX * (NX + NU) * 2, transcendentals=0
        ),
        name="lower_nodes",
    )(count, leaf_s, leaf_u, leafw, sc, cc)


def gather_kernel(
    parent_ref, midw_ref, value_ref, mid_s, mid_u,
    total_ref, weight_ref,
    own_buf, other_buf, sib_buf, in_buf, out_buf, tile, sib_tile, in_tile, out_tile,
    sib_send, sib_recv, send_sem, recv_sem,
):
    row = lax.axis_index("row")
    col = lax.axis_index("col")
    z = col // 2
    core = lax.rem(col, 2)
    sibling = col + 1 - 2 * core
    dist = lax.rem(z + 8 - 4 * core, 8)
    is_target = dist == 0
    down = jnp.logical_and(dist >= 1, dist <= 4)
    up_col = 2 * lax.rem(z + 1, 8) + core
    down_col = 2 * lax.rem(z + 7, 8) + core
    next_col = jnp.where(down, down_col, up_col)
    side = jnp.where(dist == 7, 1, 0)
    has_up = jnp.logical_and(dist != 4, dist != 5)

    barrier = pltpu.get_barrier_semaphore()
    for peer in (sibling, up_col, down_col):
        pl.semaphore_signal(barrier, inc=1, device_id=(row, peer), device_id_type=MESH)
    weight = midw_ref[0]
    parent = parent_ref[0]
    w_own = jnp.where(parent == core, weight, 0.0)
    w_other = jnp.where(parent == core, 0.0, weight)

    def put(i, block):
        own_buf[i * H : (i + 1) * H, :] = w_own * block
        other_buf[i * H : (i + 1) * H, :] = (w_other * block).astype(BF16)

    node_term(value_ref, mid_s.at[0], mid_u.at[0], put)
    tile[...] = jnp.where(iota2((8, 128), 0) == parent, weight, 0.0)
    pl.semaphore_wait(barrier, 3)

    def chunk(c):
        return pl.ds(pl.multiple_of(c * CHUNK, 16), CHUNK)

    def remote(src, dst, send, recv, peer):
        return pltpu.make_async_remote_copy(
            src_ref=src, dst_ref=dst, send_sem=send, recv_sem=recv,
            device_id=(row, peer), device_id_type=MESH,
        )

    def sib_copy(c):
        return remote(
            other_buf.at[chunk(c)], sib_buf.at[chunk(c)], sib_send.at[c], sib_recv.at[c], sibling
        )

    def chain_copy(c, to_side):
        return remote(
            out_buf.at[chunk(c)], in_buf.at[to_side, chunk(c)],
            send_sem.at[c], recv_sem.at[to_side, c], next_col,
        )

    def sib_tile_copy():
        return remote(tile, sib_tile, sib_send.at[N_CHUNK], sib_recv.at[N_CHUNK], sibling)

    def tile_copy(to_side):
        return remote(
            out_tile, in_tile.at[to_side],
            send_sem.at[N_CHUNK], recv_sem.at[to_side, N_CHUNK], next_col,
        )

    def start_sib(c, carry):
        sib_copy(c).start()
        return carry

    lax.fori_loop(0, N_CHUNK, start_sib, 0)
    sib_tile_copy().start()

    def step(c, carry):
        rows = chunk(c)
        sib_copy(c).wait_recv()
        part = own_buf[rows, :] + sib_buf[rows, :].astype(F32)

        @pl.when(jnp.logical_not(has_up))
        def _():
            out_buf[rows, :] = part.astype(BF16)
            chain_copy(c, side).start()

        @pl.when(has_up)
        def _():
            chain_copy(c, 0).wait_recv()
            more = part + in_buf[0, rows, :].astype(F32)

            @pl.when(is_target)
            def _():
                chain_copy(c, 1).wait_recv()
                total_ref[rows, :] = more + in_buf[1, rows, :].astype(F32)

            @pl.when(jnp.logical_not(is_target))
            def _():
                out_buf[rows, :] = more.astype(BF16)
                chain_copy(c, side).start()

        return carry

    lax.fori_loop(0, N_CHUNK, step, 0)
    sib_tile_copy().wait_recv()
    tiles = tile[...] + sib_tile[...]

    @pl.when(jnp.logical_not(has_up))
    def _():
        out_tile[...] = tiles
        tile_copy(side).start()

    @pl.when(has_up)
    def _():
        tile_copy(0).wait_recv()
        more = tiles + in_tile[0]

        @pl.when(is_target)
        def _():
            tile_copy(1).wait_recv()
            weight_ref[...] = more + in_tile[1]

        @pl.when(jnp.logical_not(is_target))
        def _():
            out_tile[...] = more
            tile_copy(side).start()

    def drain(c, carry):
        sib_copy(c).wait_send()

        @pl.when(jnp.logical_not(is_target))
        def _():
            chain_copy(c, side).wait_send()

        return carry

    lax.fori_loop(0, N_CHUNK, drain, 0)
    sib_tile_copy().wait_send()

    @pl.when(jnp.logical_not(is_target))
    def _():
        tile_copy(side).wait_send()


def gather(parent, midw, value, mid_s, mid_u):
    smem = pl.BlockSpec(memory_space=pltpu.SMEM)
    vmem = pl.BlockSpec(memory_space=pltpu.VMEM)
    dma = pltpu.SemaphoreType.DMA
    return pl.pallas_call(
        gather_kernel,
        out_shape=(
            jax.ShapeDtypeStruct((ROWS, H), F32),
            jax.ShapeDtypeStruct((8, 128), F32),
        ),
        in_specs=[smem, smem, vmem, vmem, vmem],
        out_specs=(vmem,) * 2,
        scratch_shapes=[
            pltpu.VMEM((ROWS, H), F32),
            pltpu.VMEM((ROWS, H), BF16),
            pltpu.VMEM((ROWS, H), BF16),
            pltpu.VMEM((2, ROWS, H), BF16),
            pltpu.VMEM((ROWS, H), BF16),
            pltpu.VMEM((8, 128), F32),
            pltpu.VMEM((8, 128), F32),
            pltpu.VMEM((2, 8, 128), F32),
            pltpu.VMEM((8, 128), F32),
            dma((N_CHUNK + 1,)),
            dma((N_CHUNK + 1,)),
            dma((N_CHUNK + 1,)),
            dma((2, N_CHUNK + 1)),
        ],
        compiler_params=pltpu.CompilerParams(
            collective_id=0, has_side_effects=True, vmem_limit_bytes=VMEM_LIMIT
        ),
        name="group_sum",
    )(parent, midw, value, mid_s, mid_u)


def upper_kernel(total_ref, weight_ref, sc_ref, cc_ref, gv_ref, blocks, work, feed):
    col = lax.axis_index("col")
    core = lax.rem(col, 2)

    @pl.when(col == 9 * core)
    def _():
        picked = jnp.where(iota2((8, 128), 0) == core, weight_ref[...], 0.0)
        scale = 1.0 / jnp.sum(picked, axis=0, keepdims=True)[:, :1]
        for i in range(6):
            blocks[i] = total_ref[i * H : (i + 1) * H, :] * scale
        gain_ref = gv_ref.at[pl.ds(0, NU)]
        value_ref = gv_ref.at[pl.ds(NU, NX)]
        riccati(lambda i: blocks[i], sc_ref[...], cc_ref[...], gain_ref, value_ref, work, feed)


def upper(total, weight, sc, cc):
    vmem = pl.BlockSpec(memory_space=pltpu.VMEM)
    return pl.pallas_call(
        upper_kernel,
        out_shape=jax.ShapeDtypeStruct((GV_ROWS, NX), BF16),
        in_specs=[vmem] * 4,
        out_specs=vmem,
        scratch_shapes=[
            pltpu.VMEM((6, H, H), F32),
            pltpu.VMEM((H, H), F32),
            pltpu.VMEM((NU, NX), F32),
        ],
        compiler_params=pltpu.CompilerParams(vmem_limit_bytes=VMEM_LIMIT),
        name="upper_nodes",
    )(total, weight, sc, cc)


def hops(step):
    return min(step, 4 - step)


NEAR = sorted(
    [(dy, dx) for dy in range(4) for dx in range(4) if dy or dx],
    key=lambda step: hops(step[0]) + hops(step[1]),
)


def root_kernel(
    upw_ref, gv_ref, up_s, up_u, gvs_ref, total_ref, wtiles_ref,
    term_ref, wtile_ref, in_buf, piece_buf, pair_buf,
    w_send, w_recv, ws_send, ws_recv, a_send, a_recv, b_send, b_recv, c_send, c_recv,
    s_send, s_recv, g_send, g_recv, gs_send, gs_recv,
):
    row = lax.axis_index("row")
    col = lax.axis_index("col")
    z = col // 2
    core = lax.rem(col, 2)
    sibling = col + 1 - 2 * core
    dist = lax.rem(z + 8 - 4 * core, 8)
    is_target = dist == 0
    is_adder = dist == 4
    is_plain = jnp.logical_not(jnp.logical_or(is_target, is_adder))
    up_col = 2 * lax.rem(z + 1, 8) + core
    down_col = 2 * lax.rem(z + 7, 8) + core
    other_adder = 2 * lax.rem(z + 4, 8) + 1 - core
    slot = 1 - core
    barrier = pltpu.get_barrier_semaphore()

    def signal(to_row, to_col):
        pl.semaphore_signal(barrier, inc=1, device_id=(to_row, to_col), device_id_type=MESH)

    def peers(body):
        def one(k, carry):
            body(lax.rem(row + k, 16))
            return carry

        lax.fori_loop(1, 16, one, 0)

    def at_step(step):
        return lax.rem(row // 4 + step[0], 4) * 4 + lax.rem(lax.rem(row, 4) + step[1], 4)

    def far_first(body):
        for step in reversed(NEAR):
            body(at_step(step))

    def near_first(body):
        for step in NEAR:
            body(at_step(step))

    for to_col in (sibling, up_col, down_col):
        signal(row, to_col)

    @pl.when(is_target)
    def _():
        peers(lambda p: signal(p, sibling))

    @pl.when(is_adder)
    def _():
        peers(lambda p: signal(p, sibling))
        peers(lambda p: signal(p, col))
        signal(row, other_adder)
        for off in (1, 2, 3, 5, 6, 7):
            for half in range(2):
                signal(row, 2 * lax.rem(z + off, 8) + half)

    @pl.when(is_plain)
    def _():
        peers(lambda p: signal(p, col))
        signal(row, 1)
        signal(row, 8)

    def remote(src, dst, send, recv, to_row, to_col):
        return pltpu.make_async_remote_copy(
            src_ref=src, dst_ref=dst, send_sem=send, recv_sem=recv,
            device_id=(to_row, to_col), device_id_type=MESH,
        )

    def a_copy(to_row, at):
        return remote(
            term_ref.at[pl.ds(pl.multiple_of(to_row * PIECE, 16), PIECE)], in_buf.at[at],
            a_send.at[to_row], a_recv.at[at], to_row, sibling,
        )

    def b_half(off, half, of_slot):
        return remote(
            piece_buf.at[half], pair_buf.at[of_slot, half],
            b_send.at[2 * off + half], b_recv.at[of_slot], row, 2 * lax.rem(z + off, 8) + half,
        )

    def b_whole(of_slot):
        return remote(
            piece_buf, pair_buf.at[of_slot], b_send.at[0], b_recv.at[of_slot], row, other_adder
        )

    def c_half(to_row, at):
        part = total_ref.at[at, core]
        return remote(part, part, c_send.at[to_row], c_recv.at[at], to_row, col)

    def c_whole(to_row, at):
        part = total_ref.at[at]
        return remote(part, part, c_send.at[to_row], c_recv.at[at], to_row, col)

    def s_half(at, half):
        part = total_ref.at[at, half]
        return remote(part, part, s_send.at[at], s_recv.at[at], row, sibling)

    def s_whole(at):
        part = total_ref.at[at]
        return remote(part, part, s_send.at[at], s_recv.at[at], row, sibling)

    def w_copy(to_row, at):
        return remote(wtile_ref, wtiles_ref.at[at], w_send.at[to_row], w_recv.at[at], to_row, col)

    def ws_copy():
        return remote(wtiles_ref, wtiles_ref, ws_send.at[0], ws_recv.at[0], row, sibling)

    def g_part(c, of_slot):
        return gvs_ref.at[of_slot, pl.ds(pl.multiple_of(c * GV_CHUNK, 16), GV_CHUNK)]

    def g_copy(c, to_col, way):
        part = g_part(c, core)
        return remote(part, part, g_send.at[way, c], g_recv.at[c], row, to_col)

    def gs_copy(c, of_slot):
        part = g_part(c, of_slot)
        return remote(part, part, gs_send.at[c], gs_recv.at[c], row, sibling)

    def gv_chunks(body, first=0, last=N_GV):
        def one(c, carry):
            body(c)
            return carry

        lax.fori_loop(first, last, one, 0)

    to_up = dist <= 3
    to_down = jnp.logical_or(dist == 0, dist >= 6)

    def forward(c):
        @pl.when(to_up)
        def _():
            g_copy(c, up_col, 0).start()

        @pl.when(to_down)
        def _():
            g_copy(c, down_col, 1).start()

        gs_copy(c, core).start()

    def relay(c):
        g_copy(c, up_col, 0).wait_recv()
        forward(c)

    def pieces(body):
        def one(at, carry):
            body(at)
            return carry

        lax.fori_loop(0, 16, one, 0)

    def send_tiles():
        peers(lambda p: w_copy(p, row).start())
        wtiles_ref[pl.ds(row, 1)] = wtile_ref[...][None]

    wtile_ref[...] = jnp.full((8, 128), upw_ref[0] + upw_ref[1], F32)

    @pl.when(is_target)
    def _():
        gvs_ref[pl.ds(core, 1)] = gv_ref[...][None]
        up_weight = jnp.where(core == 0, upw_ref[0], upw_ref[1])
        pl.semaphore_wait(barrier, 18)
        gv_chunks(forward)

        def put(i, block):
            term_ref[i * H : (i + 1) * H, :] = (up_weight * block).astype(BF16)

        node_term(gv_ref.at[pl.ds(NU, NX)], up_s.at[core], up_u.at[core], put)
        far_first(lambda p: a_copy(p, row).start())
        a_copy(row, row).start()

    @pl.when(is_adder)
    def _():
        pl.semaphore_wait(barrier, 46)

    @pl.when(is_plain)
    def _():
        pl.semaphore_wait(barrier, 20)

    @pl.when(is_target)
    def _():
        pieces(lambda at: s_whole(at).wait_recv())
        ws_copy().wait_recv()
        pieces(lambda p: a_copy(p, row).wait_send())

    @pl.when(is_adder)
    def _():
        send_tiles()
        a_copy(row, row).wait_recv()
        acc = in_buf[row].astype(F32)
        for step in NEAR:
            source = at_step(step)
            a_copy(source, source).wait_recv()
            acc = acc + in_buf[source].astype(F32)
        piece = acc.astype(BF16)
        piece_buf[0] = piece[:HALF]
        piece_buf[1] = piece[HALF:]
        b_whole(slot).start()
        for off in (3, 5, 2, 6, 1, 7):
            for half in range(2):
                b_half(off, half, slot).start()
        own = piece_buf[...].astype(F32)
        b_whole(core).wait_recv()
        pair = own + pair_buf[core].astype(F32)
        total_ref[pl.ds(row, 1)] = pair.astype(BF16)[None]
        far_first(lambda p: c_whole(p, row).start())
        s_whole(row).start()
        def relay_piece(p):
            c_whole(p, p).wait_recv()
            s_whole(p).start()

        near_first(relay_piece)
        gv_chunks(relay)
        peers(lambda p: w_copy(p, p).wait_recv())
        ws_copy().start()
        ws_copy().wait_send()
        pieces(lambda at: s_whole(at).wait_send())
        peers(lambda p: c_whole(p, row).wait_send())
        peers(lambda p: w_copy(p, row).wait_send())
        b_whole(slot).wait_send()
        for off in (3, 5, 2, 6, 1, 7):
            for half in range(2):
                b_half(off, half, slot).wait_send()

    steps = jnp.minimum(dist, 8 - dist)
    early = jnp.where(steps <= 2, N_GV, N_GV // 2)

    @pl.when(is_plain)
    def _():
        send_tiles()
        gv_chunks(relay, 0, early)
        b_half(1, core, 0).wait_recv()
        b_half(1, core, 1).wait_recv()
        pair = pair_buf[0, core].astype(F32) + pair_buf[1, core].astype(F32)
        total_ref[pl.ds(row, 1), pl.ds(core, 1)] = pair.astype(BF16)[None, None]
        far_first(lambda p: c_half(p, row).start())
        s_half(row, core).start()
        gv_chunks(relay, early, N_GV)

        def relay_piece(p):
            c_half(p, p).wait_recv()
            s_half(p, core).start()

        near_first(relay_piece)

        def finish(at):
            s_half(at, 1 - core).wait_recv()
            s_half(at, core).wait_send()

        pieces(finish)
        peers(lambda p: w_copy(p, p).wait_recv())
        peers(lambda p: c_half(p, row).wait_send())
        peers(lambda p: w_copy(p, row).wait_send())

    def finish_gv(c):
        gs_copy(c, 1 - core).wait_recv()
        gs_copy(c, core).wait_send()

        @pl.when(to_up)
        def _():
            g_copy(c, up_col, 0).wait_send()

        @pl.when(to_down)
        def _():
            g_copy(c, down_col, 1).wait_send()

    gv_chunks(finish_gv)


def root_sum(upw, gv, up_s, up_u):
    smem = pl.BlockSpec(memory_space=pltpu.SMEM)
    vmem = pl.BlockSpec(memory_space=pltpu.VMEM)
    dma = pltpu.SemaphoreType.DMA
    return pl.pallas_call(
        root_kernel,
        out_shape=(
            jax.ShapeDtypeStruct((2, GV_ROWS, NX), BF16),
            jax.ShapeDtypeStruct((16, 2, HALF, H), BF16),
            jax.ShapeDtypeStruct((16, 8, 128), F32),
        ),
        in_specs=[smem, vmem, vmem, vmem],
        out_specs=(vmem,) * 3,
        scratch_shapes=[
            pltpu.VMEM((ROWS, H), BF16),
            pltpu.VMEM((8, 128), F32),
            pltpu.VMEM((16, PIECE, H), BF16),
            pltpu.VMEM((2, HALF, H), BF16),
            pltpu.VMEM((2, 2, HALF, H), BF16),
            dma((16,)), dma((16,)),
            dma((1,)), dma((1,)),
            dma((16,)), dma((16,)),
            dma((16,)), dma((2,)),
            dma((16,)), dma((16,)),
            dma((16,)), dma((16,)),
            dma((2, N_GV)), dma((N_GV,)),
            dma((N_GV,)), dma((N_GV,)),
        ],
        compiler_params=pltpu.CompilerParams(
            collective_id=1, has_side_effects=True, vmem_limit_bytes=VMEM_LIMIT
        ),
        name="root_sum",
    )(upw, gv, up_s, up_u)


def down_kernel(
    count_ref, parent_ref, gvs_ref, total_ref, wtiles_ref, mid_gain_ref, mid_value_ref, root_cov_ref,
    up_s, up_u, mid_s, mid_u, leaf_s, leaf_u, sc_ref, cc_ref, nc_ref,
    root_gain_out, root_value_out, up_gain_out, up_value_out, up_cov_out,
    mid_gain_out, mid_value_out, mid_cov_out, leaf_cov_out,
    root_gain_ref, root_value_ref, up_cov_ref, mid_cov_ref, lcov, blocks, work, feed, out_sems,
):
    outs = []

    def emit(src, dst):
        copy = pltpu.make_async_copy(src, dst, out_sems.at[len(outs)])
        copy.start()
        outs.append(copy)

    for s in range(2):
        emit(gvs_ref.at[s, pl.ds(0, NU)], up_gain_out.at[s])
        emit(gvs_ref.at[s, pl.ds(NU, NX)], up_value_out.at[s])
    emit(mid_gain_ref, mid_gain_out)
    emit(mid_value_ref, mid_value_out)
    weight = jnp.sum(wtiles_ref[...], axis=0)
    scale = 1.0 / weight[:1, :1]
    for i in range(6):
        blocks[i] = total_ref[i * H : (i + 1) * H, :].astype(F32) * scale
    riccati(
        lambda i: blocks[i], sc_ref[...], cc_ref[...], root_gain_ref, root_value_ref, work, feed
    )
    emit(root_gain_ref, root_gain_out)
    emit(root_value_ref, root_value_out)
    noise = nc_ref[...]
    root_gain = root_gain_ref[...]
    root_cov = root_cov_ref[...]
    for s in range(2):
        store_cov(up_cov_ref.at[s], propagate(root_cov, root_gain, up_s[s], up_u[s], noise))
        emit(up_cov_ref.at[s], up_cov_out.at[s])
    parent = parent_ref[0]
    store_cov(
        mid_cov_ref,
        propagate(up_cov_ref[parent], gvs_ref[parent, :NU, :], mid_s[0], mid_u[0], noise),
    )
    emit(mid_cov_ref, mid_cov_out)
    live = count_ref[0]
    mid_cov = mid_cov_ref[...]
    mid_gain = mid_gain_ref[...]
    for c in range(LEAF):
        keep = c < live
        result = propagate(mid_cov, mid_gain, leaf_s[c], leaf_u[c], noise)
        store_cov(lcov.at[c], [jnp.where(keep, block, jnp.zeros_like(block)) for block in result])
        emit(lcov.at[c], leaf_cov_out.at[c])
    for out in outs:
        out.wait()


def down(count, parent, *arrays):
    smem = pl.BlockSpec(memory_space=pltpu.SMEM)
    vmem = pl.BlockSpec(memory_space=pltpu.VMEM)
    hbm = pl.BlockSpec(memory_space=pl.ANY)
    return pl.pallas_call(
        down_kernel,
        out_shape=(
            jax.ShapeDtypeStruct((NU, NX), BF16),
            jax.ShapeDtypeStruct((NX, NX), BF16),
            jax.ShapeDtypeStruct((2, NU, NX), BF16),
            jax.ShapeDtypeStruct((2, NX, NX), BF16),
            jax.ShapeDtypeStruct((2, NX, NX), BF16),
            jax.ShapeDtypeStruct((NU, NX), BF16),
            jax.ShapeDtypeStruct((NX, NX), BF16),
            jax.ShapeDtypeStruct((NX, NX), BF16),
            jax.ShapeDtypeStruct((LEAF, NX, NX), BF16),
        ),
        in_specs=[smem, smem] + [vmem] * len(arrays),
        out_specs=(hbm,) * 9,
        scratch_shapes=[
            pltpu.VMEM((NU, NX), BF16),
            pltpu.VMEM((NX, NX), BF16),
            pltpu.VMEM((2, NX, NX), BF16),
            pltpu.VMEM((NX, NX), BF16),
            pltpu.VMEM((LEAF, NX, NX), BF16),
            pltpu.VMEM((6, H, H), F32),
            pltpu.VMEM((H, H), F32),
            pltpu.VMEM((NU, NX), F32),
            pltpu.SemaphoreType.DMA((15,)),
        ],
        compiler_params=pltpu.CompilerParams(vmem_limit_bytes=VMEM_LIMIT),
        name="down_sweep",
    )(count, parent, *arrays)


def local(
    leaf_state_map,
    leaf_input_map,
    leaf_weight,
    leaf_count,
    mid_state_map,
    mid_input_map,
    mid_weight,
    mid_parent,
    up_state_map,
    up_input_map,
    up_weight,
    root_cov,
    state_cost,
    control_cost,
    noise_cov,
):
    sc = state_cost.reshape(1, NX)
    cc = control_cost.reshape(1, NU)
    nc = noise_cov.reshape(1, NX)
    mid_gain, mid_value = lower(
        leaf_count, leaf_state_map, leaf_input_map, leaf_weight.reshape(1, LEAF), sc, cc
    )
    total, weight = gather(mid_parent, mid_weight, mid_value, mid_state_map, mid_input_map)
    gv = upper(total, weight, sc, cc)
    gvs, root_total, wtiles = root_sum(up_weight, gv, up_state_map, up_input_map)
    outs = down(
        leaf_count, mid_parent, gvs, root_total.reshape(ROWS, H), wtiles, mid_gain, mid_value,
        root_cov, up_state_map, up_input_map, mid_state_map, mid_input_map,
        leaf_state_map, leaf_input_map, sc, cc, nc,
    )
    root_gain, root_value, up_gain, up_value, up_cov, mid_gain, mid_value, mid_cov, leaf_cov = outs
    return (
        root_gain,
        root_value,
        up_gain,
        up_value,
        up_cov,
        mid_gain[None],
        mid_value[None],
        mid_cov[None],
        leaf_cov,
    )


def solution(mesh):
    both = P(("row", "col"))
    return jax.shard_map(
        local,
        mesh=mesh,
        in_specs=(
            both, both, both, both, both, both, both, both,
            P("row"), P("row"), P("row"), P(), P(), P(), P(),
        ),
        out_specs=(P(), P(), P("row"), P("row"), P("row"), both, both, both, both),
        check_vma=False,
    )
```
